256 devices in a mesh: head: 4 (over y), seq: 16 (over z, core), ctx: 4 (over x).
Axes of the slice: x: 4, y: 4, z: 8, core: 2. Of those that a mesh axis runs over, the one named last changes fastest.
Arguments:
- queries: bfloat16 [128, 256, 2048], P(('seq', 'ctx'), 'head'), may hold values from -96 to 96
- keys: bfloat16 [128, 256, 2048], P(('seq', 'ctx'), 'head'), may hold values from -6 to 6
- values: bfloat16 [128, 256, 2048], P(('seq', 'ctx'), 'head'), may hold values from -6 to 6
- cotangent: bfloat16 [128, 256, 2048], P(('seq', 'ctx'), 'head'), may hold values from -6 to 6
Outputs:
- attended: bfloat16 [128, 256, 2048], P(('seq', 'ctx'), 'head')
- grad_queries: bfloat16 [128, 256, 2048], P(('seq', 'ctx'), 'head')
- grad_keys: bfloat16 [128, 256, 2048], P(('seq', 'ctx'), 'head')
- grad_values: bfloat16 [128, 256, 2048], P(('seq', 'ctx'), 'head')
The draws below stay inside these ranges and needn't reach their ends.
All inputs are finite; a program needn't handle non-finite values.
Results may differ from the reference program's by a relative error of at most 0.0075.
Values may be sent and summed in bfloat16 or wider, within the bound.
No kernel may reach another device: no remote copies, remote signals or barrier semaphores. Data moves between devices by JAX's collectives and lax.ppermute only.
A program may use at most 64 MiB of HBM per device.

```python
import math
import jax
import jax.numpy as jnp
import numpy as np
from jax import lax

HEADS = 16
HD = 128
BLOCK = 256
NBLK = 128


def common_keys(key):
    return jnp.clip(jax.random.normal(key, (NBLK * BLOCK, HEADS * HD), jnp.float32), -6.0, 6.0)


def draw_keys(key, part):
    base = common_keys(key)
    return base.reshape(NBLK, BLOCK, HEADS * HD).astype(jnp.bfloat16)


def draw_queries(key, part):
    key = jax.random.fold_in(key, 12)
    fresh = jnp.clip(jax.random.normal(key, (NBLK * BLOCK, HEADS * HD), jnp.float32), -6.0, 6.0)
    return fresh.reshape(NBLK, BLOCK, HEADS * HD).astype(jnp.bfloat16)


def steps_of(stream_key, dims, shards, low, largest):
    def one(dim, parts):
        draws = jax.random.uniform(jax.random.fold_in(jax.random.fold_in(stream_key, 6), dim), (parts,), jnp.float32, low / len(shards), largest / len(shards))
        return jnp.repeat(jnp.exp(draws), dims[dim] // parts).reshape((-1,) + (1,) * (len(dims) - dim - 1))

    level = one(*shards[0])
    for cut in shards[1:]:
        level = level * one(*cut)
    return level


def bell_draw(stream_key, extent, scale, reach, shards=(), kind=jnp.bfloat16):
    gain = steps_of(stream_key, extent, shards, -0.22, 0.18) if shards else 1.0
    drawn = jax.random.normal(stream_key, extent, jnp.float32) * scale * gain
    return jnp.minimum(jnp.maximum(drawn, -reach), reach).astype(kind)


def setup_inputs(seed: int = 0) -> dict:
    key_list = jax.random.split(jax.random.key(seed), 5)
    queries = draw_queries(jax.random.fold_in(key_list[4], 71), 0)
    keys = draw_keys(jax.random.fold_in(key_list[4], 71), 0)
    values = bell_draw(key_list[2], (NBLK, BLOCK, HEADS * HD), 1.0, 6.0, ((0, 64), (1, 4)))
    cotangent = bell_draw(key_list[3], (NBLK, BLOCK, HEADS * HD), 1.0, 6.0, ((0, 64), (1, 4)))
    return {"queries": queries, "keys": keys, "values": values, "cotangent": cotangent}


def key_offsets(block_rows):
    counts = [block_rows, block_rows, block_rows // 2, block_rows // 2] + [block_rows // 4] * 4
    return np.repeat(np.arange(8), counts).astype(np.int32)

def allowed_mask(block_index, block_rows):
    offsets = jnp.asarray(key_offsets(block_rows))
    row_ids = jnp.arange(block_rows, dtype=jnp.int32)
    col_ids = jnp.arange(offsets.shape[0], dtype=jnp.int32)
    usable = block_index - offsets >= 0
    causal = (offsets != 0)[None, :] | (col_ids[None, :] <= row_ids[:, None])
    return usable[None, :] & causal

def pooled(source, factor):
    n_rows, features = source.shape
    return source.astype(jnp.float32).reshape(n_rows // factor, factor, features).mean(axis=1).astype(jnp.bfloat16)

def unpooled(grads, factor):
    n_rows, features = grads.shape
    spread = jnp.broadcast_to(grads[:, None, :] * (1.0 / factor), (n_rows, factor, features))
    return spread.reshape(n_rows * factor, features)

def head_core(queries, cotangent, keyset, valset, allowed):
    score_scale = 1.0 / math.sqrt(queries.shape[1])
    scores = jnp.dot(queries, keyset.T, preferred_element_type=jnp.float32) * score_scale
    scores = jnp.where(allowed, scores, -1e+30)
    row_max = lax.optimization_barrier(jnp.max(scores, axis=1, keepdims=True))
    exp_scores = jnp.exp(scores - row_max)
    weights = (exp_scores / lax.optimization_barrier(jnp.sum(exp_scores, axis=1, keepdims=True))).astype(jnp.bfloat16)
    output = jnp.dot(weights, valset, preferred_element_type=jnp.float32).astype(jnp.bfloat16)
    dweights = jnp.dot(cotangent, valset.T, preferred_element_type=jnp.float32)
    wfloat = weights.astype(jnp.float32)
    row_delta = lax.optimization_barrier(jnp.sum(wfloat * dweights, axis=1, keepdims=True))
    dscores = (wfloat * (dweights - row_delta) * score_scale).astype(jnp.bfloat16)
    dquery = jnp.dot(dscores, keyset, preferred_element_type=jnp.float32).astype(jnp.bfloat16)
    dkeys = jnp.dot(dscores.T, queries, preferred_element_type=jnp.float32)
    dvals = jnp.dot(weights.T, cotangent, preferred_element_type=jnp.float32)
    return (output, dquery, dkeys, dvals)

def block_core(queries, cotangent, keyset, valset, allowed, head_dim):
    head_count = queries.shape[1] // head_dim

    def split_heads(source):
        return source.reshape(source.shape[0], head_count, head_dim).transpose(1, 0, 2)

    def join_heads(source):
        return source.transpose(1, 0, 2).reshape(source.shape[1], head_count * head_dim)

    def per_head(members):
        return head_core(members[0], members[1], members[2], members[3], allowed)
    results = lax.map(per_head, (split_heads(queries), split_heads(cotangent), split_heads(keyset), split_heads(valset)))
    return tuple((join_heads(result) for result in results))

def reference(queries, keys, values, cotangent):
    block_count, block_rows, features = queries.shape
    half = block_rows // 2
    quarter = block_rows // 4
    mid_keys = pooled(keys.reshape(-1, features), 2).reshape(block_count, half, features)
    mid_vals = pooled(values.reshape(-1, features), 2).reshape(block_count, half, features)
    far_keys = pooled(keys.reshape(-1, features), 4).reshape(block_count, quarter, features)
    far_vals = pooled(values.reshape(-1, features), 4).reshape(block_count, quarter, features)

    def piece_at(stack, block_index, offset):
        source = block_index - offset
        chosen = stack[jnp.maximum(source, 0)]
        return jnp.where(source >= 0, chosen, jnp.zeros_like(chosen))

    def one_block(block_index):
        key_parts = [keys[block_index], piece_at(keys, block_index, 1), piece_at(mid_keys, block_index, 2), piece_at(mid_keys, block_index, 3)]
        key_parts = key_parts + [piece_at(far_keys, block_index, offset) for offset in range(4, 8)]
        val_parts = [values[block_index], piece_at(values, block_index, 1), piece_at(mid_vals, block_index, 2), piece_at(mid_vals, block_index, 3)]
        val_parts = val_parts + [piece_at(far_vals, block_index, offset) for offset in range(4, 8)]
        keyset = jnp.concatenate(key_parts, axis=0)
        valset = jnp.concatenate(val_parts, axis=0)
        allowed = allowed_mask(block_index, block_rows)
        return block_core(queries[block_index], cotangent[block_index], keyset, valset, allowed, HD)
    outputs, dqueries, dkeyset, dvalset = lax.map(one_block, jnp.arange(block_count, dtype=jnp.int32))

    def received(stack, offset):
        return jnp.concatenate([stack[offset:], jnp.zeros_like(stack[:offset])], axis=0)

    def owner_grads(stack):
        base = 2 * block_rows
        farbase = 3 * block_rows
        fine = stack[:, :block_rows] + received(stack[:, block_rows:base], 1)
        middle = received(stack[:, base:base + half], 2) + received(stack[:, base + half:farbase], 3)
        distant = received(stack[:, farbase:farbase + quarter], 4)
        for offset in range(5, 8):
            start = farbase + (offset - 4) * quarter
            distant = distant + received(stack[:, start:start + quarter], offset)
        total = fine + jax.vmap(lambda grads: unpooled(grads, 2))(middle) + jax.vmap(lambda grads: unpooled(grads, 4))(distant)
        return total.astype(jnp.bfloat16)
    return (outputs, dqueries, owner_grads(dkeyset), owner_grads(dvalset))
```

```python
import functools
import math

import jax
import jax.numpy as jnp
from jax import lax
from jax.experimental import pallas as pl
from jax.experimental.pallas import tpu as pltpu
from jax.sharding import PartitionSpec as P

HD = 128
BLOCK = 256
HALF = BLOCK // 2
QUARTER = BLOCK // 4
SCALE = 1.0 / math.sqrt(HD)
LOG2E = 1.0 / math.log(2.0)
NEG = -1e30
HALO_FINE = BLOCK
HALO_MID = 2 * HALF
HALO_FAR = 6 * QUARTER
HALO = HALO_FINE + HALO_MID + HALO_FAR
BACK = BLOCK + 2 * HALF + 4 * QUARTER
GROUP_AXES = ("ctx", "head")
VMEM = 48 * 1024 * 1024


def whole(count):
    return [pl.BlockSpec(memory_space=pltpu.VMEM)] * count


def params():
    return pltpu.CompilerParams(vmem_limit_bytes=VMEM)


def cost(flops, nbytes):
    return pl.CostEstimate(flops=flops, bytes_accessed=nbytes, transcendentals=0)


def spread_body(first, second, out):
    for head in range(out.shape[0]):
        out[head, 0] = first[:, :, head * HD : (head + 1) * HD]
        out[head, 1] = second[:, :, head * HD : (head + 1) * HD]


def spread(first, second):
    blocks, rows, features = first.shape
    heads = features // HD
    return pl.pallas_call(
        spread_body,
        out_shape=jax.ShapeDtypeStruct((heads, 2, blocks, rows, HD), first.dtype),
        in_specs=whole(2),
        out_specs=whole(1)[0],
        compiler_params=params(),
        cost_estimate=cost(0, 4 * first.size * 2),
    )(first, second)


def join_body(moved, first, second):
    for head in range(moved.shape[0]):
        first[:, :, head * HD : (head + 1) * HD] = moved[head, 0]
        second[:, :, head * HD : (head + 1) * HD] = moved[head, 1]


def join(moved):
    heads, _, blocks, rows, _ = moved.shape
    out = jax.ShapeDtypeStruct((blocks, rows, heads * HD), moved.dtype)
    return pl.pallas_call(
        join_body,
        out_shape=(out, out),
        in_specs=whole(1),
        out_specs=tuple(whole(2)),
        compiler_params=params(),
        cost_estimate=cost(0, 2 * moved.size * 2),
    )(moved)


def pool_matrix():
    row = lax.broadcasted_iota(jnp.int32, (HALF + QUARTER, BLOCK), 0)
    col = lax.broadcasted_iota(jnp.int32, (HALF + QUARTER, BLOCK), 1)
    pair = (row < HALF) & ((col >> 1) == row)
    four = (row >= HALF) & ((col >> 2) == row - HALF)
    both = jnp.where(pair, 0.5, 0.0) + jnp.where(four, 0.25, 0.0)
    return both.astype(jnp.bfloat16)


def pool_body(moved, fine, mid, far, msg):
    sources, _, local, rows, _ = moved.shape
    per_block = BLOCK // rows
    blocks = sources // per_block * local
    matrix = pool_matrix()
    for kv in range(2):
        for block in range(blocks):
            first = block // local * per_block
            tokens = jnp.concatenate(
                [moved[first + part, kv, block % local] for part in range(per_block)], axis=0
            )
            pooled = jnp.dot(matrix, tokens, preferred_element_type=jnp.float32)
            pooled = pooled.astype(jnp.bfloat16)
            fine[kv, block * BLOCK : (block + 1) * BLOCK] = tokens
            mid[kv, block * HALF : (block + 1) * HALF] = pooled[:HALF]
            far[kv, block * QUARTER : (block + 1) * QUARTER] = pooled[HALF:]
            from_end = blocks - block
            if from_end == 1:
                msg[kv, :HALO_FINE] = tokens
            if from_end in (2, 3):
                start = HALO_FINE + (3 - from_end) * HALF
                msg[kv, start : start + HALF] = pooled[:HALF]
            if 2 <= from_end <= 7:
                start = HALO_FINE + HALO_MID + (7 - from_end) * QUARTER
                msg[kv, start : start + QUARTER] = pooled[HALF:]


def pool(moved):
    sources, _, local, rows, _ = moved.shape
    blocks = sources * rows // BLOCK * local
    shape = functools.partial(jax.ShapeDtypeStruct, dtype=jnp.bfloat16)
    return pl.pallas_call(
        pool_body,
        out_shape=(
            shape((2, blocks * BLOCK, HD)),
            shape((2, blocks * HALF, HD)),
            shape((2, blocks * QUARTER, HD)),
            shape((2, HALO, HD)),
        ),
        in_specs=whole(1),
        out_specs=tuple(whole(4)),
        compiler_params=params(),
        cost_estimate=cost(4 * blocks * 192 * BLOCK * HD, moved.size * 6),
    )(moved)


def dot_nt(a, b):
    return lax.dot_general(a, b, (((1,), (1,)), ((), ())), preferred_element_type=jnp.float32)


def dot_tn(a, b):
    return lax.dot_general(a, b, (((0,), (0,)), ((), ())), preferred_element_type=jnp.float32)


def dot_nn(a, b):
    return jnp.dot(a, b, preferred_element_type=jnp.float32)


def attend_body(
    first_group, moved, fine, mid, far, halo, out, total, back, fext, mext, rext, fgrad, mgrad, rgrad
):
    sources, _, local, rows, _ = moved.shape
    per_block = BLOCK // rows
    blocks = sources // per_block * local
    matrix = pool_matrix()
    for kv in range(2):
        tokens = halo[kv, :HALO_FINE]
        pooled = jnp.dot(matrix, tokens, preferred_element_type=jnp.float32).astype(jnp.bfloat16)
        fext[kv, :BLOCK] = tokens
        fext[kv, BLOCK:] = fine[kv]
        mext[kv, : 2 * HALF] = halo[kv, HALO_FINE : HALO_FINE + HALO_MID]
        mext[kv, 2 * HALF : 3 * HALF] = pooled[:HALF]
        mext[kv, 3 * HALF :] = mid[kv]
        rext[kv, : 6 * QUARTER] = halo[kv, HALO_FINE + HALO_MID :]
        rext[kv, 6 * QUARTER : 7 * QUARTER] = pooled[HALF:]
        rext[kv, 7 * QUARTER :] = far[kv]
    fgrad[...] = jnp.zeros_like(fgrad)
    mgrad[...] = jnp.zeros_like(mgrad)
    rgrad[...] = jnp.zeros_like(rgrad)
    is_first = first_group[0]

    def one_block(step, inner):
        block = step * local + inner
        fine_at = pl.ds(pl.multiple_of(block * BLOCK, BLOCK), 2 * BLOCK)
        mid_at = pl.ds(pl.multiple_of(block * HALF, HALF), 2 * HALF)
        far_at = pl.ds(pl.multiple_of(block * QUARTER, QUARTER), 4 * QUARTER)

        def window(kv):
            return jnp.concatenate([fext[kv, fine_at], mext[kv, mid_at], rext[kv, far_at]], axis=0)

        def chunk(which):
            return jnp.concatenate(
                [moved[step * per_block + part, which, inner] for part in range(per_block)], axis=0
            )

        queries = chunk(0)
        cotangent = chunk(1)
        keyset = window(0)
        valset = window(1)
        scores = dot_nt(keyset, queries)
        row = lax.broadcasted_iota(jnp.int32, (BLOCK, BLOCK), 0)
        col = lax.broadcasted_iota(jnp.int32, (BLOCK, BLOCK), 1)
        absent = is_first * jnp.maximum(1 - block, 0) * BLOCK
        absent_mid = is_first * jnp.maximum(3 - block, 0) * HALF
        absent_far = is_first * jnp.maximum(7 - block, 0) * QUARTER
        scores = jnp.concatenate(
            [
                jnp.where(row < absent, NEG, scores[:BLOCK]),
                jnp.where(row <= col, scores[BLOCK : 2 * BLOCK], NEG),
                jnp.where(row < absent_mid, NEG, scores[2 * BLOCK : 3 * BLOCK]),
                jnp.where(row < absent_far, NEG, scores[3 * BLOCK :]),
            ],
            axis=0,
        )
        factor = SCALE * LOG2E
        top = jnp.max(scores, axis=0, keepdims=True)
        powers = jnp.exp2((scores - top) * factor)
        norm = 1.0 / jnp.sum(powers, axis=0, keepdims=True)
        weights = powers * norm
        weights_low = weights.astype(jnp.bfloat16)
        attended = dot_tn(valset, weights_low)
        turned = jnp.transpose(cotangent.astype(jnp.float32))
        delta = jnp.sum(attended * turned, axis=0, keepdims=True)
        dweights = dot_nt(valset, cotangent)
        dscores = (weights * (dweights - delta)).astype(jnp.bfloat16)
        dqueries = dot_tn(keyset, dscores) * SCALE
        dkeys = dot_nn(dscores, queries) * SCALE
        dvalues = dot_nn(weights_low, cotangent)
        attended_rows = jnp.transpose(attended).astype(jnp.bfloat16)
        dqueries_rows = jnp.transpose(dqueries).astype(jnp.bfloat16)
        for part in range(per_block):
            at = slice(part * rows, (part + 1) * rows)
            out[step * per_block + part, 0, inner] = attended_rows[at]
            out[step * per_block + part, 1, inner] = dqueries_rows[at]
        for kv, grads in enumerate((dkeys, dvalues)):
            fgrad[kv, fine_at] += grads[: 2 * BLOCK]
            mgrad[kv, mid_at] += grads[2 * BLOCK : 3 * BLOCK]
            rgrad[kv, far_at] += grads[3 * BLOCK :]

    def steps(step, carry):
        for inner in range(local):
            one_block(step, inner)
        return carry

    lax.fori_loop(0, blocks // local, steps, 0)

    for kv in range(2):
        pairs = mgrad[kv, 2 * HALF :] * 0.5
        fours = rgrad[kv, 6 * QUARTER :] * 0.25
        for lane in range(2):
            fgrad[kv, pl.ds(lane, (blocks + 1) * HALF, stride=2), :] += pairs
        for lane in range(4):
            fgrad[kv, pl.ds(lane, (blocks + 1) * QUARTER, stride=4), :] += fours
        shares = rgrad[kv, 4 * QUARTER : 6 * QUARTER] * 0.5
        for lane in range(2):
            mgrad[kv, pl.ds(lane, 2 * QUARTER, stride=2), :] += shares
        total[kv] = fgrad[kv, BLOCK:]
        back[kv, :BLOCK] = fgrad[kv, :BLOCK].astype(jnp.bfloat16)
        back[kv, BLOCK : BLOCK + 2 * HALF] = mgrad[kv, : 2 * HALF].astype(jnp.bfloat16)
        back[kv, BLOCK + 2 * HALF :] = rgrad[kv, : 4 * QUARTER].astype(jnp.bfloat16)


def attend(first_group, moved, fine, mid, far, halo):
    tokens = fine.shape[1]
    blocks = tokens // BLOCK
    f32 = jnp.float32
    flops = blocks * 6 * 2 * BLOCK * 4 * BLOCK * HD
    return pl.pallas_call(
        attend_body,
        out_shape=(
            jax.ShapeDtypeStruct(moved.shape, moved.dtype),
            jax.ShapeDtypeStruct((2, tokens, HD), f32),
            jax.ShapeDtypeStruct((2, BACK, HD), jnp.bfloat16),
        ),
        in_specs=[pl.BlockSpec(memory_space=pltpu.SMEM)] + whole(5),
        out_specs=tuple(whole(3)),
        scratch_shapes=[
            pltpu.VMEM((2, (blocks + 1) * BLOCK, HD), jnp.bfloat16),
            pltpu.VMEM((2, (blocks + 3) * HALF, HD), jnp.bfloat16),
            pltpu.VMEM((2, (blocks + 7) * QUARTER, HD), jnp.bfloat16),
            pltpu.VMEM((2, (blocks + 1) * BLOCK, HD), f32),
            pltpu.VMEM((2, (blocks + 3) * HALF, HD), f32),
            pltpu.VMEM((2, (blocks + 7) * QUARTER, HD), f32),
        ],
        compiler_params=params(),
        cost_estimate=cost(flops, 6 * 2**20),
    )(first_group, moved, fine, mid, far, halo)


def finish_body(total, back, out, scratch):
    sources, _, local, rows, _ = out.shape
    per_block = BLOCK // rows
    blocks = sources // per_block * local
    for kv in range(2):
        scratch[...] = total[kv]
        last = (blocks - 1) * BLOCK
        scratch[last:] += back[kv, :BLOCK].astype(jnp.float32)
        pairs = back[kv, BLOCK : BLOCK + 2 * HALF].astype(jnp.float32) * 0.5
        for lane in range(2):
            at = pl.ds((blocks - 3) * BLOCK + lane, 2 * HALF, stride=2)
            scratch[at, :] += pairs
        fours = back[kv, BLOCK + 2 * HALF :].astype(jnp.float32) * 0.25
        for lane in range(4):
            at = pl.ds((blocks - 7) * BLOCK + lane, 4 * QUARTER, stride=4)
            scratch[at, :] += fours
        for block in range(blocks):
            for part in range(per_block):
                start = block * BLOCK + part * rows
                source = block // local * per_block + part
                out[source, kv, block % local] = scratch[start : start + rows].astype(jnp.bfloat16)


def finish(total, back, shape):
    return pl.pallas_call(
        finish_body,
        out_shape=jax.ShapeDtypeStruct(shape, jnp.bfloat16),
        in_specs=whole(2),
        out_specs=whole(1)[0],
        scratch_shapes=[pltpu.VMEM(total.shape[1:], jnp.float32)],
        compiler_params=params(),
        cost_estimate=cost(0, total.size * 6),
    )(total, back)


def exchange(parts):
    return lax.all_to_all(parts, GROUP_AXES, split_axis=0, concat_axis=0, tiled=True)


def shifted(block, distance):
    devices = range(lax.axis_size("seq"))
    route = [(i - distance, i) for i in devices if i - distance in devices]
    return lax.ppermute(block, "seq", route)


def shards(queries, keys, values, cotangent):
    with jax.named_scope("keys_in"):
        moved_kv = exchange(spread(keys, values))
    with jax.named_scope("queries_in"):
        sent = spread(queries, cotangent)
        sent, moved_kv = lax.optimization_barrier((sent, moved_kv))
        moved_qc = exchange(sent)
    with jax.named_scope("halo"):
        fine, mid, far, msg = pool(moved_kv)
        halo = shifted(msg, 1)
    first_group = (lax.axis_index("seq") == 0).astype(jnp.int32).reshape(1)
    with jax.named_scope("attend"):
        out, total, back = attend(first_group, moved_qc, fine, mid, far, halo)
    with jax.named_scope("outputs_back"):
        moved_out = exchange(out)
    with jax.named_scope("halo_back"):
        received = shifted(back, -1)
        grads = finish(total, received, moved_kv.shape)
    with jax.named_scope("grads_back"):
        grads, moved_out = lax.optimization_barrier((grads, moved_out))
        moved_grads = exchange(grads)
    attended, grad_queries = join(moved_out)
    grad_keys, grad_values = join(moved_grads)
    return (attended, grad_queries, grad_keys, grad_values)


def solution(mesh):
    spec = P(("seq", "ctx"), "head", None)
    return jax.shard_map(
        shards, mesh=mesh, in_specs=(spec,) * 4, out_specs=(spec,) * 4, check_vma=False
    )
```

```python
import functools
import math

import jax
import jax.numpy as jnp
from jax import lax
from jax.experimental import pallas as pl
from jax.experimental.pallas import tpu as pltpu
from jax.sharding import PartitionSpec as P

HD = 128
BLOCK = 256
HALF = BLOCK // 2
QUARTER = BLOCK // 4
SCALE = 1.0 / math.sqrt(HD)
LOG2E = 1.0 / math.log(2.0)
NEG = -1e30
HALO_FINE = BLOCK
HALO_MID = 2 * HALF
HALO_FAR = 6 * QUARTER
HALO = HALO_FINE + HALO_MID + HALO_FAR
BACK = BLOCK + 2 * HALF + 4 * QUARTER
GROUP_AXES = ("ctx", "head")


def whole(count):
    return [pl.BlockSpec(memory_space=pltpu.VMEM)] * count


def params(mebibytes):
    return pltpu.CompilerParams(vmem_limit_bytes=mebibytes * 2**20)


def cost(flops, nbytes):
    return pl.CostEstimate(flops=flops, bytes_accessed=nbytes, transcendentals=0)


def spread_body(*refs):
    count = (len(refs) - 2) // 2
    sources, out, held, sems = refs[:count], refs[count], refs[count + 1 : -1], refs[-1]
    blocks = out.shape[2]
    copies = {}
    for which in range(count):
        for block in range(blocks):
            copies[which, block] = pltpu.make_async_copy(
                sources[which].at[block], held[which].at[block], sems.at[which, block]
            )
            copies[which, block].start()
    for which in range(count):
        for block in range(blocks):
            copies[which, block].wait()
            for head in range(out.shape[0]):
                out[head, which, block] = held[which][block, :, head * HD : (head + 1) * HD]


def spread(*arrays):
    blocks, rows, features = arrays[0].shape
    heads = features // HD
    count = len(arrays)
    return pl.pallas_call(
        spread_body,
        out_shape=jax.ShapeDtypeStruct((heads, count, blocks, rows, HD), arrays[0].dtype),
        in_specs=[pl.BlockSpec(memory_space=pltpu.HBM)] * count,
        out_specs=whole(1)[0],
        scratch_shapes=[pltpu.VMEM((blocks, rows, features), arrays[0].dtype)] * count
        + [pltpu.SemaphoreType.DMA((count, blocks))],
        compiler_params=params(58),
        cost_estimate=cost(0, 4 * count * arrays[0].size),
    )(*arrays)


def join_body(moved, *outs):
    for which, out in enumerate(outs):
        for head in range(moved.shape[0]):
            out[:, :, head * HD : (head + 1) * HD] = moved[head, which]


def join(moved):
    heads, count, blocks, rows, _ = moved.shape
    out = jax.ShapeDtypeStruct((blocks, rows, heads * HD), moved.dtype)
    return pl.pallas_call(
        join_body,
        out_shape=(out,) * count,
        in_specs=whole(1),
        out_specs=tuple(whole(count)),
        compiler_params=params(8),
        cost_estimate=cost(0, 4 * moved.size),
    )(moved)


def pool_matrix():
    row = lax.broadcasted_iota(jnp.int32, (HALF + QUARTER, BLOCK), 0)
    col = lax.broadcasted_iota(jnp.int32, (HALF + QUARTER, BLOCK), 1)
    pair = (row < HALF) & ((col >> 1) == row)
    four = (row >= HALF) & ((col >> 2) == row - HALF)
    both = jnp.where(pair, 0.5, 0.0) + jnp.where(four, 0.25, 0.0)
    return both.astype(jnp.bfloat16)


def sizes(moved):
    sources, _, local, rows, _ = moved.shape
    per_block = BLOCK // rows
    return sources // per_block * local, local, per_block, rows


def tokens_of(moved, which, step, inner):
    per_block = BLOCK // moved.shape[3]
    return jnp.concatenate(
        [moved[step * per_block + part, which, inner] for part in range(per_block)], axis=0
    )


def places(block):
    return (
        pl.ds(pl.multiple_of(block * BLOCK, BLOCK), 2 * BLOCK),
        pl.ds(pl.multiple_of(block * HALF, HALF), 2 * HALF),
        pl.ds(pl.multiple_of(block * QUARTER, QUARTER), 4 * QUARTER),
    )


def window(extended, kv, block):
    return jnp.concatenate([ref[kv, at] for ref, at in zip(extended, places(block))], axis=0)


def store_rows(out, which, step, inner, value):
    rows = out.shape[3]
    per_block = BLOCK // rows
    for part in range(per_block):
        out[step * per_block + part, which, inner] = value[part * rows : (part + 1) * rows]


def each_block(moved, one_block):
    blocks, local, _, _ = sizes(moved)

    def steps(step, carry):
        for inner in range(local):
            one_block(step, inner, step * local + inner)
        return carry

    lax.fori_loop(0, blocks // local, steps, 0)


def pooled_rows(matrix, tokens):
    return jnp.dot(matrix, tokens, preferred_element_type=jnp.float32).astype(jnp.bfloat16)


def message_body(moved, msg):
    blocks, local, _, _ = sizes(moved)
    matrix = pool_matrix()
    for kv in range(2):
        for from_end in range(1, 8):
            block = blocks - from_end
            tokens = tokens_of(moved, kv, block // local, block % local)
            if from_end == 1:
                msg[kv, :HALO_FINE] = tokens
                continue
            pooled = pooled_rows(matrix, tokens)
            if from_end <= 3:
                start = HALO_FINE + (3 - from_end) * HALF
                msg[kv, start : start + HALF] = pooled[:HALF]
            start = HALO_FINE + HALO_MID + (7 - from_end) * QUARTER
            msg[kv, start : start + QUARTER] = pooled[HALF:]


def message(moved):
    return pl.pallas_call(
        message_body,
        out_shape=jax.ShapeDtypeStruct((2, HALO, HD), jnp.bfloat16),
        in_specs=whole(1),
        out_specs=whole(1)[0],
        compiler_params=params(8),
        cost_estimate=cost(4 * 6 * 192 * BLOCK * HD, moved.size * 2),
    )(moved)


def dot_nt(a, b):
    return lax.dot_general(a, b, (((1,), (1,)), ((), ())), preferred_element_type=jnp.float32)


def dot_tn(a, b):
    return lax.dot_general(a, b, (((0,), (0,)), ((), ())), preferred_element_type=jnp.float32)


def dot_nn(a, b):
    return jnp.dot(a, b, preferred_element_type=jnp.float32)


def extend(moved, halo, fext, mext, rext):
    blocks, local, _, _ = sizes(moved)
    matrix = pool_matrix()
    for kv in range(2):
        mext[kv, : 2 * HALF] = halo[kv, HALO_FINE : HALO_FINE + HALO_MID]
        rext[kv, : 6 * QUARTER] = halo[kv, HALO_FINE + HALO_MID :]
        for block in range(-1, blocks):
            if block < 0:
                tokens = halo[kv, :HALO_FINE]
            else:
                tokens = tokens_of(moved, kv, block // local, block % local)
            pooled = pooled_rows(matrix, tokens)
            fext[kv, (block + 1) * BLOCK : (block + 2) * BLOCK] = tokens
            mext[kv, (block + 3) * HALF : (block + 4) * HALF] = pooled[:HALF]
            rext[kv, (block + 7) * QUARTER : (block + 8) * QUARTER] = pooled[HALF:]


def attend_body(
    first_group,
    moved,
    moved_kv,
    halo,
    out,
    total,
    back,
    fext,
    mext,
    rext,
    fgrad,
    mgrad,
    rgrad,
):
    blocks, local, per_block, rows = sizes(moved)
    extend(moved_kv, halo, fext, mext, rext)
    fgrad[...] = jnp.zeros_like(fgrad)
    mgrad[...] = jnp.zeros_like(mgrad)
    rgrad[...] = jnp.zeros_like(rgrad)
    is_first = first_group[0]
    extended = (fext, mext, rext)

    def one_block(step, inner, block):
        queries = tokens_of(moved, 0, step, inner)
        cotangent = tokens_of(moved, 1, step, inner)
        keyset = window(extended, 0, block)
        valset = window(extended, 1, block)
        scores = dot_nt(keyset, queries)
        row = lax.broadcasted_iota(jnp.int32, (BLOCK, BLOCK), 0)
        col = lax.broadcasted_iota(jnp.int32, (BLOCK, BLOCK), 1)
        absent = is_first * jnp.maximum(1 - block, 0) * BLOCK
        absent_mid = is_first * jnp.maximum(3 - block, 0) * HALF
        absent_far = is_first * jnp.maximum(7 - block, 0) * QUARTER
        scores = jnp.concatenate(
            [
                jnp.where(row < absent, NEG, scores[:BLOCK]),
                jnp.where(row <= col, scores[BLOCK : 2 * BLOCK], NEG),
                jnp.where(row < absent_mid, NEG, scores[2 * BLOCK : 3 * BLOCK]),
                jnp.where(row < absent_far, NEG, scores[3 * BLOCK :]),
            ],
            axis=0,
        )
        top = jnp.max(scores, axis=0, keepdims=True)
        powers = jnp.exp2((scores - top) * (SCALE * LOG2E))
        norm = 1.0 / jnp.sum(powers, axis=0, keepdims=True)
        normed = powers * norm
        weights = normed.astype(jnp.bfloat16)
        attended = dot_tn(valset, weights)
        turned = jnp.transpose(cotangent.astype(jnp.float32))
        delta = jnp.sum(attended * turned, axis=0, keepdims=True)
        dweights = dot_nt(valset, cotangent)
        dscores = (normed * (dweights - delta)).astype(jnp.bfloat16)
        dqueries = dot_tn(keyset, dscores) * SCALE
        dkeys = dot_nn(dscores, queries) * SCALE
        dvalues = dot_nn(weights, cotangent)
        store_rows(out, 0, step, inner, jnp.transpose(attended).astype(jnp.bfloat16))
        store_rows(out, 1, step, inner, jnp.transpose(dqueries).astype(jnp.bfloat16))
        fine_at, mid_at, far_at = places(block)
        for kv, grads in enumerate((dkeys, dvalues)):
            fgrad[kv, fine_at] += grads[: 2 * BLOCK]
            mgrad[kv, mid_at] += grads[2 * BLOCK : 3 * BLOCK]
            rgrad[kv, far_at] += grads[3 * BLOCK :]

    each_block(moved, one_block)
    for kv in range(2):
        pairs = mgrad[kv, 2 * HALF :] * 0.5
        fours = rgrad[kv, 6 * QUARTER :] * 0.25
        for lane in range(2):
            fgrad[kv, pl.ds(lane, (blocks + 1) * HALF, stride=2), :] += pairs
        for lane in range(4):
            fgrad[kv, pl.ds(lane, (blocks + 1) * QUARTER, stride=4), :] += fours
        shares = rgrad[kv, 4 * QUARTER : 6 * QUARTER] * 0.5
        for lane in range(2):
            mgrad[kv, pl.ds(lane, 2 * QUARTER, stride=2), :] += shares
        total[kv] = fgrad[kv, BLOCK:]
        back[kv, :BLOCK] = fgrad[kv, :BLOCK].astype(jnp.bfloat16)
        back[kv, BLOCK : BLOCK + 2 * HALF] = mgrad[kv, : 2 * HALF].astype(jnp.bfloat16)
        back[kv, BLOCK + 2 * HALF :] = rgrad[kv, : 4 * QUARTER].astype(jnp.bfloat16)


def attend(first_group, moved, moved_kv, halo):
    blocks, local, per_block, rows = sizes(moved)
    f32 = jnp.float32
    return pl.pallas_call(
        attend_body,
        out_shape=(
            jax.ShapeDtypeStruct((moved.shape[0], 4) + moved.shape[2:], moved.dtype),
            jax.ShapeDtypeStruct((2, blocks * BLOCK, HD), f32),
            jax.ShapeDtypeStruct((2, BACK, HD), jnp.bfloat16),
        ),
        in_specs=[pl.BlockSpec(memory_space=pltpu.SMEM)] + whole(3),
        out_specs=tuple(whole(3)),
        scratch_shapes=[
            pltpu.VMEM((2, (blocks + 1) * BLOCK, HD), jnp.bfloat16),
            pltpu.VMEM((2, (blocks + 3) * HALF, HD), jnp.bfloat16),
            pltpu.VMEM((2, (blocks + 7) * QUARTER, HD), jnp.bfloat16),
            pltpu.VMEM((2, (blocks + 1) * BLOCK, HD), f32),
            pltpu.VMEM((2, (blocks + 3) * HALF, HD), f32),
            pltpu.VMEM((2, (blocks + 7) * QUARTER, HD), f32),
        ],
        compiler_params=params(24),
        cost_estimate=cost(blocks * 12 * BLOCK * 4 * BLOCK * HD, 8 * 2**20),
    )(first_group, moved, moved_kv, halo)


def finish_body(total, back, given, out, scratch):
    sources, _, local, rows, _ = out.shape
    per_block = BLOCK // rows
    blocks = sources // per_block * local
    for kv in range(2):
        scratch[...] = total[kv]
        last = (blocks - 1) * BLOCK
        scratch[last:] += back[kv, :BLOCK].astype(jnp.float32)
        pairs = back[kv, BLOCK : BLOCK + 2 * HALF].astype(jnp.float32) * 0.5
        for lane in range(2):
            at = pl.ds((blocks - 3) * BLOCK + lane, 2 * HALF, stride=2)
            scratch[at, :] += pairs
        fours = back[kv, BLOCK + 2 * HALF :].astype(jnp.float32) * 0.25
        for lane in range(4):
            at = pl.ds((blocks - 7) * BLOCK + lane, 4 * QUARTER, stride=4)
            scratch[at, :] += fours
        for source in range(sources):
            for inner in range(local):
                start = (source // per_block * local + inner) * BLOCK + source % per_block * rows
                piece = scratch[start : start + rows].astype(jnp.bfloat16)
                out[source, 2 + kv, inner] = piece


def finish(total, back, out):
    return pl.pallas_call(
        finish_body,
        out_shape=jax.ShapeDtypeStruct(out.shape, out.dtype),
        in_specs=whole(2) + [pl.BlockSpec(memory_space=pltpu.VMEM)],
        out_specs=whole(1)[0],
        scratch_shapes=[pltpu.VMEM(total.shape[1:], jnp.float32)],
        input_output_aliases={2: 0},
        compiler_params=params(12),
        cost_estimate=cost(0, total.size * 6),
    )(total, back, out)


def exchange(parts):
    return lax.all_to_all(parts, GROUP_AXES, split_axis=0, concat_axis=0, tiled=True)


def shifted(block, distance):
    devices = range(lax.axis_size("seq"))
    route = [(i - distance, i) for i in devices if i - distance in devices]
    return lax.ppermute(block, "seq", route)


def shards(queries, keys, values, cotangent):
    first_group = (lax.axis_index("seq") == 0).astype(jnp.int32).reshape(1)
    with jax.named_scope("keys_in"):
        moved_kv = exchange(spread(keys, values))
    with jax.named_scope("queries_in"):
        sent, moved_kv = lax.optimization_barrier((spread(queries, cotangent), moved_kv))
        moved = exchange(sent)
    with jax.named_scope("halo"):
        halo = shifted(message(moved_kv), 1)
    with jax.named_scope("attend"):
        out, total, back = attend(first_group, moved, moved_kv, halo)
    with jax.named_scope("halo_back"):
        out = finish(total, shifted(back, -1), out)
    with jax.named_scope("outputs"):
        return join(exchange(out))


def solution(mesh):
    spec = P(("seq", "ctx"), "head", None)
    return jax.shard_map(
        shards, mesh=mesh, in_specs=(spec,) * 4, out_specs=(spec,) * 4, check_vma=False
    )
```

```python
import functools
import math

import jax
import jax.numpy as jnp
from jax import lax
from jax.experimental import pallas as pl
from jax.experimental.pallas import tpu as pltpu
from jax.sharding import PartitionSpec as P

HD = 128
BLOCK = 256
HALF = BLOCK // 2
QUARTER = BLOCK // 4
SCALE = 1.0 / math.sqrt(HD)
LOG2E = 1.0 / math.log(2.0)
NEG = -1e30
HALO_FINE = BLOCK
HALO_MID = 2 * HALF
HALO_FAR = 6 * QUARTER
HALO = HALO_FINE + HALO_MID + HALO_FAR
BACK = BLOCK + 2 * HALF + 4 * QUARTER
GROUP_AXES = ("ctx", "head")


def whole(count):
    return [pl.BlockSpec(memory_space=pltpu.VMEM)] * count


def params(mebibytes):
    return pltpu.CompilerParams(vmem_limit_bytes=mebibytes * 2**20)


def cost(flops, nbytes):
    return pl.CostEstimate(flops=flops, bytes_accessed=nbytes, transcendentals=0)


def spread_body(*refs):
    count = (len(refs) - 2) // 2
    sources, out, held, sems = refs[:count], refs[count], refs[count + 1 : -1], refs[-1]
    blocks = out.shape[2]
    copies = {}
    for which in range(count):
        for block in range(blocks):
            copies[which, block] = pltpu.make_async_copy(
                sources[which].at[block], held[which].at[block], sems.at[which, block]
            )
            copies[which, block].start()
    for which in range(count):
        for block in range(blocks):
            copies[which, block].wait()
            for head in range(out.shape[0]):
                out[head, which, block] = held[which][block, :, head * HD : (head + 1) * HD]


def spread(*arrays):
    blocks, rows, features = arrays[0].shape
    heads = features // HD
    count = len(arrays)
    return pl.pallas_call(
        spread_body,
        out_shape=jax.ShapeDtypeStruct((heads, count, blocks, rows, HD), arrays[0].dtype),
        in_specs=[pl.BlockSpec(memory_space=pltpu.HBM)] * count,
        out_specs=whole(1)[0],
        scratch_shapes=[pltpu.VMEM((blocks, rows, features), arrays[0].dtype)] * count
        + [pltpu.SemaphoreType.DMA((count, blocks))],
        compiler_params=params(58),
        cost_estimate=cost(0, 4 * count * arrays[0].size),
    )(*arrays)


def join_body(moved, *outs):
    for which, out in enumerate(outs):
        for head in range(moved.shape[0]):
            out[:, :, head * HD : (head + 1) * HD] = moved[head, which]


def join(moved):
    heads, count, blocks, rows, _ = moved.shape
    out = jax.ShapeDtypeStruct((blocks, rows, heads * HD), moved.dtype)
    return pl.pallas_call(
        join_body,
        out_shape=(out,) * count,
        in_specs=whole(1),
        out_specs=tuple(whole(count)),
        compiler_params=params(8),
        cost_estimate=cost(0, 4 * moved.size),
    )(moved)


def pool_matrix():
    row = lax.broadcasted_iota(jnp.int32, (HALF + QUARTER, BLOCK), 0)
    col = lax.broadcasted_iota(jnp.int32, (HALF + QUARTER, BLOCK), 1)
    pair = (row < HALF) & ((col >> 1) == row)
    four = (row >= HALF) & ((col >> 2) == row - HALF)
    both = jnp.where(pair, 0.5, 0.0) + jnp.where(four, 0.25, 0.0)
    return both.astype(jnp.bfloat16)


def sizes(moved):
    sources, _, local, rows, _ = moved.shape
    per_block = BLOCK // rows
    return sources // per_block * local, local, per_block, rows


def tokens_of(moved, which, step, inner):
    per_block = BLOCK // moved.shape[3]
    return jnp.concatenate(
        [moved[step * per_block + part, which, inner] for part in range(per_block)], axis=0
    )


def places(block):
    return (
        pl.ds(block * BLOCK, 2 * BLOCK),
        pl.ds(block * HALF, 2 * HALF),
        pl.ds(block * QUARTER, 4 * QUARTER),
    )


def window(extended, kv, block):
    return jnp.concatenate([ref[kv, at] for ref, at in zip(extended, places(block))], axis=0)


def store_rows(out, which, step, inner, value):
    rows = out.shape[3]
    per_block = BLOCK // rows
    for part in range(per_block):
        out[step * per_block + part, which, inner] = value[part * rows : (part + 1) * rows]


def pooled_rows(matrix, tokens):
    return jnp.dot(matrix, tokens, preferred_element_type=jnp.float32).astype(jnp.bfloat16)


def message_body(moved, msg):
    blocks, local, _, _ = sizes(moved)
    matrix = pool_matrix()
    for kv in range(2):
        for from_end in range(1, 8):
            block = blocks - from_end
            tokens = tokens_of(moved, kv, block // local, block % local)
            if from_end == 1:
                msg[kv, :HALO_FINE] = tokens
                continue
            pooled = pooled_rows(matrix, tokens)
            if from_end <= 3:
                start = HALO_FINE + (3 - from_end) * HALF
                msg[kv, start : start + HALF] = pooled[:HALF]
            start = HALO_FINE + HALO_MID + (7 - from_end) * QUARTER
            msg[kv, start : start + QUARTER] = pooled[HALF:]


def message(moved):
    return pl.pallas_call(
        message_body,
        out_shape=jax.ShapeDtypeStruct((2, HALO, HD), jnp.bfloat16),
        in_specs=whole(1),
        out_specs=whole(1)[0],
        compiler_params=params(8),
        cost_estimate=cost(4 * 6 * 192 * BLOCK * HD, moved.size * 2),
    )(moved)


def dot_nt(a, b):
    return lax.dot_general(a, b, (((1,), (1,)), ((), ())), preferred_element_type=jnp.float32)


def dot_tn(a, b):
    return lax.dot_general(a, b, (((0,), (0,)), ((), ())), preferred_element_type=jnp.float32)


def dot_nn(a, b):
    return jnp.dot(a, b, preferred_element_type=jnp.float32)


def extend(moved, halo, fext, mext, rext):
    blocks, local, _, _ = sizes(moved)
    matrix = pool_matrix()
    for kv in range(2):
        mext[kv, : 2 * HALF] = halo[kv, HALO_FINE : HALO_FINE + HALO_MID]
        rext[kv, : 6 * QUARTER] = halo[kv, HALO_FINE + HALO_MID :]
        for block in range(-1, blocks):
            if block < 0:
                tokens = halo[kv, :HALO_FINE]
            else:
                tokens = tokens_of(moved, kv, block // local, block % local)
            pooled = pooled_rows(matrix, tokens)
            fext[kv, (block + 1) * BLOCK : (block + 2) * BLOCK] = tokens
            mext[kv, (block + 3) * HALF : (block + 4) * HALF] = pooled[:HALF]
            rext[kv, (block + 7) * QUARTER : (block + 8) * QUARTER] = pooled[HALF:]


def without_absent(piece, block, offset, rows, is_first):
    count = min(max(offset - block, 0) * rows, BLOCK)
    if count == 0:
        return piece
    row = lax.broadcasted_iota(jnp.int32, (count, BLOCK), 0)
    masked = jnp.where(row < is_first * count, NEG, piece[:count])
    return masked if count == BLOCK else jnp.concatenate([masked, piece[count:]], axis=0)


def attend_body(
    first_group,
    moved,
    moved_kv,
    halo,
    out,
    total,
    back,
    fext,
    mext,
    rext,
    fgrad,
    mgrad,
    rgrad,
):
    blocks, local, _, _ = sizes(moved)
    extend(moved_kv, halo, fext, mext, rext)
    fgrad[...] = jnp.zeros_like(fgrad)
    mgrad[...] = jnp.zeros_like(mgrad)
    rgrad[...] = jnp.zeros_like(rgrad)
    is_first = first_group[0]
    extended = (fext, mext, rext)

    def products(block):
        queries = tokens_of(moved, 0, block // local, block % local)
        cotangent = tokens_of(moved, 1, block // local, block % local)
        scores = dot_nt(window(extended, 0, block), queries)
        dweights = dot_nt(window(extended, 1, block), cotangent)
        return queries, cotangent, scores, dweights

    def softmax(block, queries, cotangent, scores, dweights):
        row = lax.broadcasted_iota(jnp.int32, (BLOCK, BLOCK), 0)
        col = lax.broadcasted_iota(jnp.int32, (BLOCK, BLOCK), 1)
        scores = jnp.concatenate(
            [
                without_absent(scores[:BLOCK], block, 1, BLOCK, is_first),
                jnp.where(row <= col, scores[BLOCK : 2 * BLOCK], NEG),
                without_absent(scores[2 * BLOCK : 3 * BLOCK], block, 3, HALF, is_first),
                without_absent(scores[3 * BLOCK :], block, 7, QUARTER, is_first),
            ],
            axis=0,
        )
        top = jnp.max(scores, axis=0, keepdims=True)
        powers = jnp.exp2((scores - top) * (SCALE * LOG2E))
        norm = 1.0 / jnp.sum(powers, axis=0, keepdims=True)
        delta = jnp.sum(powers * dweights, axis=0, keepdims=True) * norm
        weights = powers * norm
        dscores = weights * (dweights - delta)
        return queries, cotangent, weights.astype(jnp.bfloat16), dscores.astype(jnp.bfloat16)

    def results(block, queries, cotangent, weights, dscores):
        step, inner = block // local, block % local
        attended = dot_tn(window(extended, 1, block), weights)
        dqueries = dot_tn(window(extended, 0, block), dscores) * SCALE
        store_rows(out, 0, step, inner, jnp.transpose(attended).astype(jnp.bfloat16))
        store_rows(out, 1, step, inner, jnp.transpose(dqueries).astype(jnp.bfloat16))
        dkeys = dot_nn(dscores, queries) * SCALE
        dvalues = dot_nn(weights, cotangent)
        fine_at, mid_at, far_at = places(block)
        for kv, grads in enumerate((dkeys, dvalues)):
            fgrad[kv, fine_at] += grads[: 2 * BLOCK]
            mgrad[kv, mid_at] += grads[2 * BLOCK : 3 * BLOCK]
            rgrad[kv, far_at] += grads[3 * BLOCK :]

    ahead = products(0)
    behind = None
    for block in range(blocks):
        current = ahead
        if block + 1 < blocks:
            ahead = products(block + 1)
        finished = softmax(block, *current)
        if behind is not None:
            results(block - 1, *behind)
        behind = finished
    results(blocks - 1, *behind)

    for kv in range(2):
        pairs = mgrad[kv, 2 * HALF :] * 0.5
        fours = rgrad[kv, 6 * QUARTER :] * 0.25
        for lane in range(2):
            fgrad[kv, pl.ds(lane, (blocks + 1) * HALF, stride=2), :] += pairs
        for lane in range(4):
            fgrad[kv, pl.ds(lane, (blocks + 1) * QUARTER, stride=4), :] += fours
        shares = rgrad[kv, 4 * QUARTER : 6 * QUARTER] * 0.5
        for lane in range(2):
            mgrad[kv, pl.ds(lane, 2 * QUARTER, stride=2), :] += shares
        total[kv] = fgrad[kv, BLOCK:]
        back[kv, :BLOCK] = fgrad[kv, :BLOCK].astype(jnp.bfloat16)
        back[kv, BLOCK : BLOCK + 2 * HALF] = mgrad[kv, : 2 * HALF].astype(jnp.bfloat16)
        back[kv, BLOCK + 2 * HALF :] = rgrad[kv, : 4 * QUARTER].astype(jnp.bfloat16)


def attend(first_group, moved, moved_kv, halo):
    blocks, local, per_block, rows = sizes(moved)
    f32 = jnp.float32
    return pl.pallas_call(
        attend_body,
        out_shape=(
            jax.ShapeDtypeStruct((moved.shape[0], 4) + moved.shape[2:], moved.dtype),
            jax.ShapeDtypeStruct((2, blocks * BLOCK, HD), f32),
            jax.ShapeDtypeStruct((2, BACK, HD), jnp.bfloat16),
        ),
        in_specs=[pl.BlockSpec(memory_space=pltpu.SMEM)] + whole(3),
        out_specs=tuple(whole(3)),
        scratch_shapes=[
            pltpu.VMEM((2, (blocks + 1) * BLOCK, HD), jnp.bfloat16),
            pltpu.VMEM((2, (blocks + 3) * HALF, HD), jnp.bfloat16),
            pltpu.VMEM((2, (blocks + 7) * QUARTER, HD), jnp.bfloat16),
            pltpu.VMEM((2, (blocks + 1) * BLOCK, HD), f32),
            pltpu.VMEM((2, (blocks + 3) * HALF, HD), f32),
            pltpu.VMEM((2, (blocks + 7) * QUARTER, HD), f32),
        ],
        compiler_params=params(24),
        cost_estimate=cost(blocks * 12 * BLOCK * 4 * BLOCK * HD, 8 * 2**20),
    )(first_group, moved, moved_kv, halo)


def finish_body(total, back, given, out, scratch):
    sources, _, local, rows, _ = out.shape
    per_block = BLOCK // rows
    blocks = sources // per_block * local
    for kv in range(2):
        scratch[...] = total[kv]
        last = (blocks - 1) * BLOCK
        scratch[last:] += back[kv, :BLOCK].astype(jnp.float32)
        pairs = back[kv, BLOCK : BLOCK + 2 * HALF].astype(jnp.float32) * 0.5
        for lane in range(2):
            at = pl.ds((blocks - 3) * BLOCK + lane, 2 * HALF, stride=2)
            scratch[at, :] += pairs
        fours = back[kv, BLOCK + 2 * HALF :].astype(jnp.float32) * 0.25
        for lane in range(4):
            at = pl.ds((blocks - 7) * BLOCK + lane, 4 * QUARTER, stride=4)
            scratch[at, :] += fours
        for source in range(sources):
            for inner in range(local):
                start = (source // per_block * local + inner) * BLOCK + source % per_block * rows
                piece = scratch[start : start + rows].astype(jnp.bfloat16)
                out[source, 2 + kv, inner] = piece


def finish(total, back, out):
    return pl.pallas_call(
        finish_body,
        out_shape=jax.ShapeDtypeStruct(out.shape, out.dtype),
        in_specs=whole(2) + [pl.BlockSpec(memory_space=pltpu.VMEM)],
        out_specs=whole(1)[0],
        scratch_shapes=[pltpu.VMEM(total.shape[1:], jnp.float32)],
        input_output_aliases={2: 0},
        compiler_params=params(12),
        cost_estimate=cost(0, total.size * 6),
    )(total, back, out)


def exchange(parts):
    return lax.all_to_all(parts, GROUP_AXES, split_axis=0, concat_axis=0, tiled=True)


def shifted(block, distance):
    devices = range(lax.axis_size("seq"))
    route = [(i - distance, i) for i in devices if i - distance in devices]
    return lax.ppermute(block, "seq", route)


def shards(queries, keys, values, cotangent):
    first_group = (lax.axis_index("seq") == 0).astype(jnp.int32).reshape(1)
    with jax.named_scope("keys_in"):
        moved_kv = exchange(spread(keys, values))
    with jax.named_scope("queries_in"):
        sent, moved_kv = lax.optimization_barrier((spread(queries, cotangent), moved_kv))
        moved = exchange(sent)
    with jax.named_scope("halo"):
        halo = shifted(message(moved_kv), 1)
    with jax.named_scope("attend"):
        out, total, back = attend(first_group, moved, moved_kv, halo)
    with jax.named_scope("halo_back"):
        out = finish(total, shifted(back, -1), out)
    with jax.named_scope("outputs"):
        return join(exchange(out))


def solution(mesh):
    spec = P(("seq", "ctx"), "head", None)
    return jax.shard_map(
        shards, mesh=mesh, in_specs=(spec,) * 4, out_specs=(spec,) * 4, check_vma=False
    )
```

```python
import functools
import math

import jax
import jax.numpy as jnp
from jax import lax
from jax.experimental import pallas as pl
from jax.experimental.pallas import tpu as pltpu
from jax.sharding import PartitionSpec as P

HD = 128
BLOCK = 256
HALF = BLOCK // 2
QUARTER = BLOCK // 4
SCALE = 1.0 / math.sqrt(HD)
LOG2E = 1.0 / math.log(2.0)
NEG = -1e30
HALO_FINE = BLOCK
HALO_MID = 2 * HALF
HALO_FAR = 6 * QUARTER
HALO = HALO_FINE + HALO_MID + HALO_FAR
BACK = BLOCK + 2 * HALF + 4 * QUARTER
GROUP_AXES = ("ctx", "head")


def whole(count):
    return [pl.BlockSpec(memory_space=pltpu.VMEM)] * count


def params(mebibytes):
    return pltpu.CompilerParams(vmem_limit_bytes=mebibytes * 2**20)


def cost(flops, nbytes):
    return pl.CostEstimate(flops=flops, bytes_accessed=nbytes, transcendentals=0)


def spread_body(*refs):
    count = (len(refs) - 2) // 2
    sources, out, held, sems = refs[:count], refs[count], refs[count + 1 : -1], refs[-1]
    blocks = out.shape[2]
    copies = {}
    for which in range(count):
        for block in range(blocks):
            copies[which, block] = pltpu.make_async_copy(
                sources[which].at[block], held[which].at[block], sems.at[which, block]
            )
            copies[which, block].start()
    for which in range(count):
        for block in range(blocks):
            copies[which, block].wait()
            for head in range(out.shape[0]):
                out[head, which, block] = held[which][block, :, head * HD : (head + 1) * HD]


def spread(*arrays):
    blocks, rows, features = arrays[0].shape
    heads = features // HD
    count = len(arrays)
    return pl.pallas_call(
        spread_body,
        out_shape=jax.ShapeDtypeStruct((heads, count, blocks, rows, HD), arrays[0].dtype),
        in_specs=[pl.BlockSpec(memory_space=pltpu.HBM)] * count,
        out_specs=whole(1)[0],
        scratch_shapes=[pltpu.VMEM((blocks, rows, features), arrays[0].dtype)] * count
        + [pltpu.SemaphoreType.DMA((count, blocks))],
        compiler_params=params(58),
        cost_estimate=cost(0, 4 * count * arrays[0].size),
    )(*arrays)


def join_body(moved, *outs):
    for which, out in enumerate(outs):
        for head in range(moved.shape[0]):
            out[:, :, head * HD : (head + 1) * HD] = moved[head, which]


def join(moved):
    heads, count, blocks, rows, _ = moved.shape
    out = jax.ShapeDtypeStruct((blocks, rows, heads * HD), moved.dtype)
    return pl.pallas_call(
        join_body,
        out_shape=(out,) * count,
        in_specs=whole(1),
        out_specs=tuple(whole(count)),
        compiler_params=params(8),
        cost_estimate=cost(0, 4 * moved.size),
    )(moved)


def pool_matrix():
    row = lax.broadcasted_iota(jnp.int32, (HALF + QUARTER, BLOCK), 0)
    col = lax.broadcasted_iota(jnp.int32, (HALF + QUARTER, BLOCK), 1)
    pair = (row < HALF) & ((col >> 1) == row)
    four = (row >= HALF) & ((col >> 2) == row - HALF)
    both = jnp.where(pair, 0.5, 0.0) + jnp.where(four, 0.25, 0.0)
    return both.astype(jnp.bfloat16)


def sizes(moved):
    sources, _, local, rows, _ = moved.shape
    per_block = BLOCK // rows
    return sources // per_block * local, local, per_block, rows


def tokens_of(moved, which, step, inner):
    per_block = BLOCK // moved.shape[3]
    return jnp.concatenate(
        [moved[step * per_block + part, which, inner] for part in range(per_block)], axis=0
    )


def places(block):
    return (
        pl.ds(block * BLOCK, 2 * BLOCK),
        pl.ds(block * HALF, 2 * HALF),
        pl.ds(block * QUARTER, 4 * QUARTER),
    )


def window(extended, kv, block):
    return jnp.concatenate([ref[kv, at] for ref, at in zip(extended, places(block))], axis=0)


def store_rows(out, which, step, inner, value):
    rows = out.shape[3]
    per_block = BLOCK // rows
    for part in range(per_block):
        out[step * per_block + part, which, inner] = value[part * rows : (part + 1) * rows]


def pooled_rows(matrix, tokens):
    return jnp.dot(matrix, tokens, preferred_element_type=jnp.float32).astype(jnp.bfloat16)


def message_body(moved, msg):
    blocks, local, _, _ = sizes(moved)
    matrix = pool_matrix()
    for kv in range(2):
        for from_end in range(1, 8):
            block = blocks - from_end
            tokens = tokens_of(moved, kv, block // local, block % local)
            if from_end == 1:
                msg[kv, :HALO_FINE] = tokens
                continue
            pooled = pooled_rows(matrix, tokens)
            if from_end <= 3:
                start = HALO_FINE + (3 - from_end) * HALF
                msg[kv, start : start + HALF] = pooled[:HALF]
            start = HALO_FINE + HALO_MID + (7 - from_end) * QUARTER
            msg[kv, start : start + QUARTER] = pooled[HALF:]


def message(moved):
    return pl.pallas_call(
        message_body,
        out_shape=jax.ShapeDtypeStruct((2, HALO, HD), jnp.bfloat16),
        in_specs=whole(1),
        out_specs=whole(1)[0],
        compiler_params=params(8),
        cost_estimate=cost(4 * 6 * 192 * BLOCK * HD, moved.size * 2),
    )(moved)


def dot_nt(a, b):
    return lax.dot_general(a, b, (((1,), (1,)), ((), ())), preferred_element_type=jnp.float32)


def dot_tn(a, b):
    return lax.dot_general(a, b, (((0,), (0,)), ((), ())), preferred_element_type=jnp.float32)


def dot_nn(a, b):
    return jnp.dot(a, b, preferred_element_type=jnp.float32)


def extend(moved, halo, fext, mext, rext):
    blocks, local, _, _ = sizes(moved)
    matrix = pool_matrix()
    for kv in range(2):
        mext[kv, : 2 * HALF] = halo[kv, HALO_FINE : HALO_FINE + HALO_MID]
        rext[kv, : 6 * QUARTER] = halo[kv, HALO_FINE + HALO_MID :]
        for block in range(-1, blocks):
            if block < 0:
                tokens = halo[kv, :HALO_FINE]
            else:
                tokens = tokens_of(moved, kv, block // local, block % local)
            pooled = pooled_rows(matrix, tokens)
            fext[kv, (block + 1) * BLOCK : (block + 2) * BLOCK] = tokens
            mext[kv, (block + 3) * HALF : (block + 4) * HALF] = pooled[:HALF]
            rext[kv, (block + 7) * QUARTER : (block + 8) * QUARTER] = pooled[HALF:]


def without_absent(piece, block, offset, rows, is_first):
    count = min(max(offset - block, 0) * rows, BLOCK)
    if count == 0:
        return piece
    row = lax.broadcasted_iota(jnp.int32, (count, BLOCK), 0)
    masked = jnp.where(row < is_first * count, NEG, piece[:count])
    return masked if count == BLOCK else jnp.concatenate([masked, piece[count:]], axis=0)


def attend_body(
    first_group,
    moved,
    moved_kv,
    halo,
    out,
    total,
    back,
    fext,
    mext,
    rext,
    fgrad,
    mgrad,
    rgrad,
):
    blocks, local, _, _ = sizes(moved)
    extend(moved_kv, halo, fext, mext, rext)
    fgrad[...] = jnp.zeros_like(fgrad)
    mgrad[...] = jnp.zeros_like(mgrad)
    rgrad[...] = jnp.zeros_like(rgrad)
    is_first = first_group[0]
    extended = (fext, mext, rext)

    def products(block):
        queries = tokens_of(moved, 0, block // local, block % local)
        cotangent = tokens_of(moved, 1, block // local, block % local)
        scores = dot_nt(window(extended, 0, block), queries)
        dweights = dot_nt(window(extended, 1, block), cotangent)
        return queries, cotangent, scores, dweights

    def softmax(block, queries, cotangent, scores, dweights):
        row = lax.broadcasted_iota(jnp.int32, (BLOCK, BLOCK), 0)
        col = lax.broadcasted_iota(jnp.int32, (BLOCK, BLOCK), 1)
        scores = jnp.concatenate(
            [
                without_absent(scores[:BLOCK], block, 1, BLOCK, is_first),
                jnp.where(row <= col, scores[BLOCK : 2 * BLOCK], NEG),
                without_absent(scores[2 * BLOCK : 3 * BLOCK], block, 3, HALF, is_first),
                without_absent(scores[3 * BLOCK :], block, 7, QUARTER, is_first),
            ],
            axis=0,
        )
        top = jnp.max(scores, axis=0, keepdims=True)
        powers = jnp.exp2((scores - top) * (SCALE * LOG2E))
        norm = 1.0 / jnp.sum(powers, axis=0, keepdims=True)
        delta = jnp.sum(powers * dweights, axis=0, keepdims=True) * norm
        weights = powers * norm
        dscores = weights * (dweights - delta)
        return queries, cotangent, weights.astype(jnp.bfloat16), dscores.astype(jnp.bfloat16)

    def results(block, queries, cotangent, weights, dscores):
        step, inner = block // local, block % local
        attended = dot_tn(window(extended, 1, block), weights)
        dqueries = dot_tn(window(extended, 0, block), dscores) * SCALE
        store_rows(out, 0, step, inner, jnp.transpose(attended).astype(jnp.bfloat16))
        store_rows(out, 1, step, inner, jnp.transpose(dqueries).astype(jnp.bfloat16))
        dkeys = dot_nn(dscores, queries) * SCALE
        dvalues = dot_nn(weights, cotangent)
        fine_at, mid_at, far_at = places(block)
        for kv, grads in enumerate((dkeys, dvalues)):
            fgrad[kv, fine_at] += grads[: 2 * BLOCK]
            mgrad[kv, mid_at] += grads[2 * BLOCK : 3 * BLOCK]
            rgrad[kv, far_at] += grads[3 * BLOCK :]

    ahead = products(0)
    behind = None
    for block in range(blocks):
        current = ahead
        if block + 1 < blocks:
            ahead = products(block + 1)
        finished = softmax(block, *current)
        if behind is not None:
            results(block - 1, *behind)
        behind = finished
    results(blocks - 1, *behind)

    for kv in range(2):
        pairs = mgrad[kv, 2 * HALF :] * 0.5
        fours = rgrad[kv, 6 * QUARTER :] * 0.25
        for lane in range(2):
            fgrad[kv, pl.ds(lane, (blocks + 1) * HALF, stride=2), :] += pairs
        for lane in range(4):
            fgrad[kv, pl.ds(lane, (blocks + 1) * QUARTER, stride=4), :] += fours
        shares = rgrad[kv, 4 * QUARTER : 6 * QUARTER] * 0.5
        for lane in range(2):
            mgrad[kv, pl.ds(lane, 2 * QUARTER, stride=2), :] += shares
        total[kv] = fgrad[kv, BLOCK:]
        back[kv, :BLOCK] = fgrad[kv, :BLOCK].astype(jnp.bfloat16)
        back[kv, BLOCK : BLOCK + 2 * HALF] = mgrad[kv, : 2 * HALF].astype(jnp.bfloat16)
        back[kv, BLOCK + 2 * HALF :] = rgrad[kv, : 4 * QUARTER].astype(jnp.bfloat16)


def attend(first_group, moved, moved_kv, halo):
    blocks, local, per_block, rows = sizes(moved)
    f32 = jnp.float32
    return pl.pallas_call(
        attend_body,
        out_shape=(
            jax.ShapeDtypeStruct((moved.shape[0], 4) + moved.shape[2:], moved.dtype),
            jax.ShapeDtypeStruct((2, blocks * BLOCK, HD), f32),
            jax.ShapeDtypeStruct((2, BACK, HD), jnp.bfloat16),
        ),
        in_specs=[pl.BlockSpec(memory_space=pltpu.SMEM)] + whole(3),
        out_specs=tuple(whole(3)),
        scratch_shapes=[
            pltpu.VMEM((2, (blocks + 1) * BLOCK, HD), jnp.bfloat16),
            pltpu.VMEM((2, (blocks + 3) * HALF, HD), jnp.bfloat16),
            pltpu.VMEM((2, (blocks + 7) * QUARTER, HD), jnp.bfloat16),
            pltpu.VMEM((2, (blocks + 1) * BLOCK, HD), f32),
            pltpu.VMEM((2, (blocks + 3) * HALF, HD), f32),
            pltpu.VMEM((2, (blocks + 7) * QUARTER, HD), f32),
        ],
        compiler_params=params(24),
        cost_estimate=cost(blocks * 12 * BLOCK * 4 * BLOCK * HD, 8 * 2**20),
    )(first_group, moved, moved_kv, halo)


def finish_body(total, back, given, out, scratch):
    out[:, :2] = given[:, :2]
    sources, _, local, rows, _ = out.shape
    per_block = BLOCK // rows
    blocks = sources // per_block * local
    for kv in range(2):
        scratch[...] = total[kv]
        last = (blocks - 1) * BLOCK
        scratch[last:] += back[kv, :BLOCK].astype(jnp.float32)
        pairs = back[kv, BLOCK : BLOCK + 2 * HALF].astype(jnp.float32) * 0.5
        for lane in range(2):
            at = pl.ds((blocks - 3) * BLOCK + lane, 2 * HALF, stride=2)
            scratch[at, :] += pairs
        fours = back[kv, BLOCK + 2 * HALF :].astype(jnp.float32) * 0.25
        for lane in range(4):
            at = pl.ds((blocks - 7) * BLOCK + lane, 4 * QUARTER, stride=4)
            scratch[at, :] += fours
        for source in range(sources):
            for inner in range(local):
                start = (source // per_block * local + inner) * BLOCK + source % per_block * rows
                piece = scratch[start : start + rows].astype(jnp.bfloat16)
                out[source, 2 + kv, inner] = piece


def finish(total, back, out):
    return pl.pallas_call(
        finish_body,
        out_shape=jax.ShapeDtypeStruct(out.shape, out.dtype),
        in_specs=whole(2) + [pl.BlockSpec(memory_space=pltpu.VMEM)],
        out_specs=whole(1)[0],
        scratch_shapes=[pltpu.VMEM(total.shape[1:], jnp.float32)],
        input_output_aliases={2: 0},
        compiler_params=params(12),
        cost_estimate=cost(0, total.size * 6),
    )(total, back, out)


def exchange(parts):
    return lax.all_to_all(parts, GROUP_AXES, split_axis=0, concat_axis=0, tiled=True)


def shifted(block, distance):
    devices = range(lax.axis_size("seq"))
    route = [(i - distance, i) for i in devices if i - distance in devices]
    return lax.ppermute(block, "seq", route)


def shards(queries, keys, values, cotangent):
    first_group = (lax.axis_index("seq") == 0).astype(jnp.int32).reshape(1)
    with jax.named_scope("keys_in"):
        moved_kv = exchange(spread(keys, values))
    with jax.named_scope("queries_in"):
        sent, moved_kv = lax.optimization_barrier((spread(queries, cotangent), moved_kv))
        moved = exchange(sent)
    with jax.named_scope("halo"):
        halo = shifted(message(moved_kv), 1)
    with jax.named_scope("attend"):
        out, total, back = attend(first_group, moved, moved_kv, halo)
    with jax.named_scope("halo_back"):
        out = finish(total, shifted(back, -1), out)
    with jax.named_scope("outputs"):
        return join(exchange(out))


def solution(mesh):
    spec = P(("seq", "ctx"), "head", None)
    return jax.shard_map(
        shards, mesh=mesh, in_specs=(spec,) * 4, out_specs=(spec,) * 4, check_vma=False
    )
```

```python
import functools
import math

import jax
import jax.numpy as jnp
from jax import lax
from jax.experimental import pallas as pl
from jax.experimental.pallas import tpu as pltpu
from jax.sharding import PartitionSpec as P

HD = 128
BLOCK = 256
HALF = BLOCK // 2
QUARTER = BLOCK // 4
SCALE = 1.0 / math.sqrt(HD)
LOG2E = 1.0 / math.log(2.0)
NEG = -1e30
HALO_FINE = BLOCK
HALO_MID = 2 * HALF
HALO_FAR = 6 * QUARTER
HALO = HALO_FINE + HALO_MID + HALO_FAR
BACK = BLOCK + 2 * HALF + 4 * QUARTER
GROUP_AXES = ("ctx", "head")


def whole(count):
    return [pl.BlockSpec(memory_space=pltpu.VMEM)] * count


def params(mebibytes):
    return pltpu.CompilerParams(vmem_limit_bytes=mebibytes * 2**20)


def cost(flops, nbytes):
    return pl.CostEstimate(flops=flops, bytes_accessed=nbytes, transcendentals=0)


def spread_body(*refs):
    count = (len(refs) - 2) // 2
    sources, out, held, sems = refs[:count], refs[count], refs[count + 1 : -1], refs[-1]
    blocks = out.shape[2]
    copies = {}
    for which in range(count):
        for block in range(blocks):
            copies[which, block] = pltpu.make_async_copy(
                sources[which].at[block], held[which].at[block], sems.at[which, block]
            )
            copies[which, block].start()
    for which in range(count):
        for block in range(blocks):
            copies[which, block].wait()
            for head in range(out.shape[0]):
                out[head, which, block] = held[which][block, :, head * HD : (head + 1) * HD]


def spread(*arrays):
    blocks, rows, features = arrays[0].shape
    heads = features // HD
    count = len(arrays)
    return pl.pallas_call(
        spread_body,
        out_shape=jax.ShapeDtypeStruct((heads, count, blocks, rows, HD), arrays[0].dtype),
        in_specs=[pl.BlockSpec(memory_space=pltpu.HBM)] * count,
        out_specs=whole(1)[0],
        scratch_shapes=[pltpu.VMEM((blocks, rows, features), arrays[0].dtype)] * count
        + [pltpu.SemaphoreType.DMA((count, blocks))],
        compiler_params=params(58),
        cost_estimate=cost(0, 4 * count * arrays[0].size),
    )(*arrays)


def join_body(moved, *outs):
    for which, out in enumerate(outs):
        for head in range(moved.shape[0]):
            out[:, :, head * HD : (head + 1) * HD] = moved[head, which]


def join(moved):
    heads, count, blocks, rows, _ = moved.shape
    out = jax.ShapeDtypeStruct((blocks, rows, heads * HD), moved.dtype)
    return pl.pallas_call(
        join_body,
        out_shape=(out,) * count,
        in_specs=whole(1),
        out_specs=tuple(whole(count)),
        compiler_params=params(8),
        cost_estimate=cost(0, 4 * moved.size),
    )(moved)


def pool_matrix():
    row = lax.broadcasted_iota(jnp.int32, (HALF + QUARTER, BLOCK), 0)
    col = lax.broadcasted_iota(jnp.int32, (HALF + QUARTER, BLOCK), 1)
    pair = (row < HALF) & ((col >> 1) == row)
    four = (row >= HALF) & ((col >> 2) == row - HALF)
    both = jnp.where(pair, 0.5, 0.0) + jnp.where(four, 0.25, 0.0)
    return both.astype(jnp.bfloat16)


def sizes(moved):
    sources, _, local, rows, _ = moved.shape
    per_block = BLOCK // rows
    return sources // per_block * local, local, per_block, rows


def tokens_of(moved, which, step, inner):
    per_block = BLOCK // moved.shape[3]
    return jnp.concatenate(
        [moved[step * per_block + part, which, inner] for part in range(per_block)], axis=0
    )


def places(block):
    return (
        pl.ds(block * BLOCK, 2 * BLOCK),
        pl.ds(block * HALF, 2 * HALF),
        pl.ds(block * QUARTER, 4 * QUARTER),
    )


def window(extended, kv, block):
    return jnp.concatenate([ref[kv, at] for ref, at in zip(extended, places(block))], axis=0)


def store_rows(out, which, step, inner, value):
    rows = out.shape[3]
    per_block = BLOCK // rows
    for part in range(per_block):
        out[step * per_block + part, which, inner] = value[part * rows : (part + 1) * rows]


def pooled_rows(matrix, tokens):
    return jnp.dot(matrix, tokens, preferred_element_type=jnp.float32).astype(jnp.bfloat16)


def message_body(moved, msg):
    blocks, local, _, _ = sizes(moved)
    matrix = pool_matrix()
    for kv in range(2):
        for from_end in range(1, 8):
            block = blocks - from_end
            tokens = tokens_of(moved, kv, block // local, block % local)
            if from_end == 1:
                msg[kv, :HALO_FINE] = tokens
                continue
            pooled = pooled_rows(matrix, tokens)
            if from_end <= 3:
                start = HALO_FINE + (3 - from_end) * HALF
                msg[kv, start : start + HALF] = pooled[:HALF]
            start = HALO_FINE + HALO_MID + (7 - from_end) * QUARTER
            msg[kv, start : start + QUARTER] = pooled[HALF:]


def message(moved):
    return pl.pallas_call(
        message_body,
        out_shape=jax.ShapeDtypeStruct((2, HALO, HD), jnp.bfloat16),
        in_specs=whole(1),
        out_specs=whole(1)[0],
        compiler_params=params(8),
        cost_estimate=cost(4 * 6 * 192 * BLOCK * HD, moved.size * 2),
    )(moved)


def dot_nt(a, b):
    return lax.dot_general(a, b, (((1,), (1,)), ((), ())), preferred_element_type=jnp.float32)


def dot_tn(a, b):
    return lax.dot_general(a, b, (((0,), (0,)), ((), ())), preferred_element_type=jnp.float32)


def dot_nn(a, b):
    return jnp.dot(a, b, preferred_element_type=jnp.float32)


def extend(moved, halo, fext, mext, rext):
    blocks, local, _, _ = sizes(moved)
    matrix = pool_matrix()
    for kv in range(2):
        mext[kv, : 2 * HALF] = halo[kv, HALO_FINE : HALO_FINE + HALO_MID]
        rext[kv, : 6 * QUARTER] = halo[kv, HALO_FINE + HALO_MID :]
        for block in range(-1, blocks):
            if block < 0:
                tokens = halo[kv, :HALO_FINE]
            else:
                tokens = tokens_of(moved, kv, block // local, block % local)
            pooled = pooled_rows(matrix, tokens)
            fext[kv, (block + 1) * BLOCK : (block + 2) * BLOCK] = tokens
            mext[kv, (block + 3) * HALF : (block + 4) * HALF] = pooled[:HALF]
            rext[kv, (block + 7) * QUARTER : (block + 8) * QUARTER] = pooled[HALF:]


def without_absent(piece, block, offset, rows, is_first):
    count = min(max(offset - block, 0) * rows, BLOCK)
    if count == 0:
        return piece
    row = lax.broadcasted_iota(jnp.int32, (count, BLOCK), 0)
    masked = jnp.where(row < is_first * count, NEG, piece[:count])
    return masked if count == BLOCK else jnp.concatenate([masked, piece[count:]], axis=0)


def attend_body(
    first_group,
    moved,
    moved_kv,
    halo,
    out,
    total,
    back,
    fext,
    mext,
    rext,
    edge,
    mgrad,
    rgrad,
):
    blocks, local, _, _ = sizes(moved)
    extend(moved_kv, halo, fext, mext, rext)
    is_first = first_group[0]
    extended = (fext, mext, rext)

    def products(block):
        queries = tokens_of(moved, 0, block // local, block % local)
        cotangent = tokens_of(moved, 1, block // local, block % local)
        scores = dot_nt(window(extended, 0, block), queries)
        dweights = dot_nt(window(extended, 1, block), cotangent)
        return queries, cotangent, scores, dweights

    def softmax(block, queries, cotangent, scores, dweights):
        row = lax.broadcasted_iota(jnp.int32, (BLOCK, BLOCK), 0)
        col = lax.broadcasted_iota(jnp.int32, (BLOCK, BLOCK), 1)
        scores = jnp.concatenate(
            [
                without_absent(scores[:BLOCK], block, 1, BLOCK, is_first),
                jnp.where(row <= col, scores[BLOCK : 2 * BLOCK], NEG),
                without_absent(scores[2 * BLOCK : 3 * BLOCK], block, 3, HALF, is_first),
                without_absent(scores[3 * BLOCK :], block, 7, QUARTER, is_first),
            ],
            axis=0,
        )
        top = jnp.max(scores, axis=0, keepdims=True)
        powers = jnp.exp2((scores - top) * (SCALE * LOG2E))
        norm = 1.0 / jnp.sum(powers, axis=0, keepdims=True)
        delta = jnp.sum(powers * dweights, axis=0, keepdims=True) * norm
        weights = powers * norm
        dscores = weights * (dweights - delta)
        return queries, cotangent, weights.astype(jnp.bfloat16), dscores.astype(jnp.bfloat16)

    def results(block, queries, cotangent, weights, dscores):
        step, inner = block // local, block % local
        attended = dot_tn(window(extended, 1, block), weights)
        dqueries = dot_tn(window(extended, 0, block), dscores) * SCALE
        store_rows(out, 0, step, inner, jnp.transpose(attended).astype(jnp.bfloat16))
        store_rows(out, 1, step, inner, jnp.transpose(dqueries).astype(jnp.bfloat16))
        dkeys = dot_nn(dscores, queries) * SCALE
        dvalues = dot_nn(weights, cotangent)
        for kv, grads in enumerate((dkeys, dvalues)):
            before, here = grads[:BLOCK], grads[BLOCK : 2 * BLOCK]
            pairs, fours = grads[2 * BLOCK : 3 * BLOCK], grads[3 * BLOCK :]
            total[kv, block * BLOCK : (block + 1) * BLOCK] = here
            if block == 0:
                edge[kv] = before
                mgrad[kv, : 2 * HALF] = pairs
                rgrad[kv, : 4 * QUARTER] = fours
                continue
            total[kv, (block - 1) * BLOCK : block * BLOCK] += before
            mgrad[kv, block * HALF : (block + 1) * HALF] += pairs[:HALF]
            mgrad[kv, (block + 1) * HALF : (block + 2) * HALF] = pairs[HALF:]
            rgrad[kv, block * QUARTER : (block + 3) * QUARTER] += fours[: 3 * QUARTER]
            rgrad[kv, (block + 3) * QUARTER : (block + 4) * QUARTER] = fours[3 * QUARTER :]

    ahead = products(0)
    behind = None
    for block in range(blocks):
        current = ahead
        if block + 1 < blocks:
            ahead = products(block + 1)
        finished = softmax(block, *current)
        if behind is not None:
            results(block - 1, *behind)
        behind = finished
    results(blocks - 1, *behind)

    for kv in range(2):
        pairs = mgrad[kv, 2 * HALF :] * 0.5
        for lane in range(2):
            edge[kv, pl.ds(lane, HALF, stride=2), :] += pairs[:HALF]
            total[kv, pl.ds(lane, (blocks - 2) * HALF, stride=2), :] += pairs[HALF:]
        fours = rgrad[kv, 6 * QUARTER :] * 0.25
        for lane in range(4):
            edge[kv, pl.ds(lane, QUARTER, stride=4), :] += fours[:QUARTER]
            total[kv, pl.ds(lane, (blocks - 4) * QUARTER, stride=4), :] += fours[QUARTER:]
        shares = rgrad[kv, 4 * QUARTER : 6 * QUARTER] * 0.5
        for lane in range(2):
            mgrad[kv, pl.ds(lane, 2 * QUARTER, stride=2), :] += shares
        back[kv, :BLOCK] = edge[kv].astype(jnp.bfloat16)
        back[kv, BLOCK : BLOCK + 2 * HALF] = mgrad[kv, : 2 * HALF].astype(jnp.bfloat16)
        back[kv, BLOCK + 2 * HALF :] = rgrad[kv, : 4 * QUARTER].astype(jnp.bfloat16)


def attend(first_group, moved, moved_kv, halo):
    blocks, local, per_block, rows = sizes(moved)
    f32 = jnp.float32
    return pl.pallas_call(
        attend_body,
        out_shape=(
            jax.ShapeDtypeStruct((moved.shape[0], 4) + moved.shape[2:], moved.dtype),
            jax.ShapeDtypeStruct((2, blocks * BLOCK, HD), f32),
            jax.ShapeDtypeStruct((2, BACK, HD), jnp.bfloat16),
        ),
        in_specs=[pl.BlockSpec(memory_space=pltpu.SMEM)] + whole(3),
        out_specs=tuple(whole(3)),
        scratch_shapes=[
            pltpu.VMEM((2, (blocks + 1) * BLOCK, HD), jnp.bfloat16),
            pltpu.VMEM((2, (blocks + 3) * HALF, HD), jnp.bfloat16),
            pltpu.VMEM((2, (blocks + 7) * QUARTER, HD), jnp.bfloat16),
            pltpu.VMEM((2, BLOCK, HD), f32),
            pltpu.VMEM((2, (blocks + 1) * HALF, HD), f32),
            pltpu.VMEM((2, (blocks + 3) * QUARTER, HD), f32),
        ],
        compiler_params=params(24),
        cost_estimate=cost(blocks * 12 * BLOCK * 4 * BLOCK * HD, 8 * 2**20),
    )(first_group, moved, moved_kv, halo)


def finish_body(total, back, given, out, scratch):
    out[:, :2] = given[:, :2]
    sources, _, local, rows, _ = out.shape
    per_block = BLOCK // rows
    blocks = sources // per_block * local
    for kv in range(2):
        scratch[...] = total[kv]
        last = (blocks - 1) * BLOCK
        scratch[last:] += back[kv, :BLOCK].astype(jnp.float32)
        pairs = back[kv, BLOCK : BLOCK + 2 * HALF].astype(jnp.float32) * 0.5
        for lane in range(2):
            at = pl.ds((blocks - 3) * BLOCK + lane, 2 * HALF, stride=2)
            scratch[at, :] += pairs
        fours = back[kv, BLOCK + 2 * HALF :].astype(jnp.float32) * 0.25
        for lane in range(4):
            at = pl.ds((blocks - 7) * BLOCK + lane, 4 * QUARTER, stride=4)
            scratch[at, :] += fours
        for source in range(sources):
            for inner in range(local):
                start = (source // per_block * local + inner) * BLOCK + source % per_block * rows
                piece = scratch[start : start + rows].astype(jnp.bfloat16)
                out[source, 2 + kv, inner] = piece


def finish(total, back, out):
    return pl.pallas_call(
        finish_body,
        out_shape=jax.ShapeDtypeStruct(out.shape, out.dtype),
        in_specs=whole(2) + [pl.BlockSpec(memory_space=pltpu.VMEM)],
        out_specs=whole(1)[0],
        scratch_shapes=[pltpu.VMEM(total.shape[1:], jnp.float32)],
        input_output_aliases={2: 0},
        compiler_params=params(12),
        cost_estimate=cost(0, total.size * 6),
    )(total, back, out)


def exchange(parts):
    return lax.all_to_all(parts, GROUP_AXES, split_axis=0, concat_axis=0, tiled=True)


def shifted(block, distance):
    devices = range(lax.axis_size("seq"))
    route = [(i - distance, i) for i in devices if i - distance in devices]
    return lax.ppermute(block, "seq", route)


def shards(queries, keys, values, cotangent):
    first_group = (lax.axis_index("seq") == 0).astype(jnp.int32).reshape(1)
    with jax.named_scope("keys_in"):
        moved_kv = exchange(spread(keys, values))
    with jax.named_scope("queries_in"):
        sent, moved_kv = lax.optimization_barrier((spread(queries, cotangent), moved_kv))
        moved = exchange(sent)
    with jax.named_scope("halo"):
        halo = shifted(message(moved_kv), 1)
    with jax.named_scope("attend"):
        out, total, back = attend(first_group, moved, moved_kv, halo)
    with jax.named_scope("halo_back"):
        out = finish(total, shifted(back, -1), out)
    with jax.named_scope("outputs"):
        return join(exchange(out))


def solution(mesh):
    spec = P(("seq", "ctx"), "head", None)
    return jax.shard_map(
        shards, mesh=mesh, in_specs=(spec,) * 4, out_specs=(spec,) * 4, check_vma=False
    )
```

```python
import functools
import math

import jax
import jax.numpy as jnp
from jax import lax
from jax.experimental import pallas as pl
from jax.experimental.pallas import tpu as pltpu
from jax.sharding import PartitionSpec as P

HD = 128
BLOCK = 256
HALF = BLOCK // 2
QUARTER = BLOCK // 4
SCALE = 1.0 / math.sqrt(HD)
LOG2E = 1.0 / math.log(2.0)
NEG = -1e30
HALO_FINE = BLOCK
HALO_MID = 2 * HALF
HALO_FAR = 6 * QUARTER
HALO = HALO_FINE + HALO_MID + HALO_FAR
BACK = BLOCK + 2 * HALF + 4 * QUARTER
GROUP_AXES = ("ctx", "head")


def whole(count):
    return [pl.BlockSpec(memory_space=pltpu.VMEM)] * count


def params(mebibytes):
    return pltpu.CompilerParams(vmem_limit_bytes=mebibytes * 2**20)


def cost(flops, nbytes):
    return pl.CostEstimate(flops=flops, bytes_accessed=nbytes, transcendentals=0)


def spread_body(*refs):
    count = (len(refs) - 2) // 3
    sources, out = refs[:count], refs[count]
    held, turned, sems = refs[count + 1 : 2 * count + 1], refs[2 * count + 1 : -1], refs[-1]
    heads, _, blocks, _, _ = out.shape
    fetches = {}
    for which in range(count):
        for block in range(blocks):
            fetches[which, block] = pltpu.make_async_copy(
                sources[which].at[block], held[which].at[block], sems.at[which, block]
            )
            fetches[which, block].start()
    sends = []
    for which in range(count):
        for block in range(blocks):
            fetches[which, block].wait()
            for head in range(heads):
                turned[which][head, block] = held[which][block, :, head * HD : (head + 1) * HD]
        send = pltpu.make_async_copy(turned[which], out.at[:, which], sems.at[which, blocks])
        send.start()
        sends.append(send)
    for send in sends:
        send.wait()


def spread(*arrays):
    blocks, rows, features = arrays[0].shape
    heads = features // HD
    count = len(arrays)
    kind = arrays[0].dtype
    there = pl.BlockSpec(memory_space=pltpu.HBM)
    return pl.pallas_call(
        spread_body,
        out_shape=jax.ShapeDtypeStruct((heads, count, blocks, rows, HD), kind),
        in_specs=[there] * count,
        out_specs=there,
        scratch_shapes=[pltpu.VMEM((blocks, rows, features), kind)] * count
        + [pltpu.VMEM((heads, blocks, rows, HD), kind)] * count
        + [pltpu.SemaphoreType.DMA((count, blocks + 1))],
        compiler_params=params(58),
        cost_estimate=cost(0, 4 * count * arrays[0].size),
    )(*arrays)


def join_body(moved, *outs):
    block = pl.program_id(0)
    for which, out in enumerate(outs):
        for head in range(moved.shape[0]):
            out[0, :, head * HD : (head + 1) * HD] = moved[head, which, block]


def join(moved):
    heads, count, blocks, rows, _ = moved.shape
    out = jax.ShapeDtypeStruct((blocks, rows, heads * HD), moved.dtype)
    one = pl.BlockSpec((1, rows, heads * HD), lambda block: (block, 0, 0))
    return pl.pallas_call(
        join_body,
        grid=(blocks,),
        out_shape=(out,) * count,
        in_specs=whole(1),
        out_specs=(one,) * count,
        compiler_params=params(8),
        cost_estimate=cost(0, 4 * moved.size),
    )(moved)


def pool_matrix():
    row = lax.broadcasted_iota(jnp.int32, (HALF + QUARTER, BLOCK), 0)
    col = lax.broadcasted_iota(jnp.int32, (HALF + QUARTER, BLOCK), 1)
    pair = (row < HALF) & ((col >> 1) == row)
    four = (row >= HALF) & ((col >> 2) == row - HALF)
    both = jnp.where(pair, 0.5, 0.0) + jnp.where(four, 0.25, 0.0)
    return both.astype(jnp.bfloat16)


def sizes(moved):
    sources, _, local, rows, _ = moved.shape
    per_block = BLOCK // rows
    return sources // per_block * local, local, per_block, rows


def tokens_of(moved, which, step, inner):
    per_block = BLOCK // moved.shape[3]
    return jnp.concatenate(
        [moved[step * per_block + part, which, inner] for part in range(per_block)], axis=0
    )


def places(block):
    return (
        pl.ds(block * BLOCK, 2 * BLOCK),
        pl.ds(block * HALF, 2 * HALF),
        pl.ds(block * QUARTER, 4 * QUARTER),
    )


def window(extended, kv, block):
    return jnp.concatenate([ref[kv, at] for ref, at in zip(extended, places(block))], axis=0)


def store_rows(out, which, step, inner, value):
    rows = out.shape[3]
    per_block = BLOCK // rows
    for part in range(per_block):
        out[step * per_block + part, which, inner] = value[part * rows : (part + 1) * rows]


def pooled_rows(matrix, tokens):
    return jnp.dot(matrix, tokens, preferred_element_type=jnp.float32).astype(jnp.bfloat16)


def message_body(moved, msg):
    blocks, local, _, _ = sizes(moved)
    matrix = pool_matrix()
    for kv in range(2):
        for from_end in range(1, 8):
            block = blocks - from_end
            tokens = tokens_of(moved, kv, block // local, block % local)
            if from_end == 1:
                msg[kv, :HALO_FINE] = tokens
                continue
            pooled = pooled_rows(matrix, tokens)
            if from_end <= 3:
                start = HALO_FINE + (3 - from_end) * HALF
                msg[kv, start : start + HALF] = pooled[:HALF]
            start = HALO_FINE + HALO_MID + (7 - from_end) * QUARTER
            msg[kv, start : start + QUARTER] = pooled[HALF:]


def message(moved):
    return pl.pallas_call(
        message_body,
        out_shape=jax.ShapeDtypeStruct((2, HALO, HD), jnp.bfloat16),
        in_specs=whole(1),
        out_specs=whole(1)[0],
        compiler_params=params(8),
        cost_estimate=cost(4 * 6 * 192 * BLOCK * HD, moved.size * 2),
    )(moved)


def dot_nt(a, b):
    return lax.dot_general(a, b, (((1,), (1,)), ((), ())), preferred_element_type=jnp.float32)


def dot_tn(a, b):
    return lax.dot_general(a, b, (((0,), (0,)), ((), ())), preferred_element_type=jnp.float32)


def dot_nn(a, b):
    return jnp.dot(a, b, preferred_element_type=jnp.float32)


def extend(moved, halo, fext, mext, rext):
    blocks, local, _, _ = sizes(moved)
    matrix = pool_matrix()
    for kv in range(2):
        mext[kv, : 2 * HALF] = halo[kv, HALO_FINE : HALO_FINE + HALO_MID]
        rext[kv, : 6 * QUARTER] = halo[kv, HALO_FINE + HALO_MID :]
        for block in range(-1, blocks):
            if block < 0:
                tokens = halo[kv, :HALO_FINE]
            else:
                tokens = tokens_of(moved, kv, block // local, block % local)
            pooled = pooled_rows(matrix, tokens)
            fext[kv, (block + 1) * BLOCK : (block + 2) * BLOCK] = tokens
            mext[kv, (block + 3) * HALF : (block + 4) * HALF] = pooled[:HALF]
            rext[kv, (block + 7) * QUARTER : (block + 8) * QUARTER] = pooled[HALF:]


def without_absent(piece, block, offset, rows, is_first):
    count = min(max(offset - block, 0) * rows, BLOCK)
    if count == 0:
        return piece
    row = lax.broadcasted_iota(jnp.int32, (count, BLOCK), 0)
    masked = jnp.where(row < is_first * count, NEG, piece[:count])
    return masked if count == BLOCK else jnp.concatenate([masked, piece[count:]], axis=0)


def attend_body(
    first_group,
    moved,
    moved_kv,
    halo,
    out,
    total,
    back,
    fext,
    mext,
    rext,
    edge,
    mgrad,
    rgrad,
):
    blocks, local, _, _ = sizes(moved)
    extend(moved_kv, halo, fext, mext, rext)
    is_first = first_group[0]
    extended = (fext, mext, rext)

    def products(block):
        queries = tokens_of(moved, 0, block // local, block % local)
        cotangent = tokens_of(moved, 1, block // local, block % local)
        scores = dot_nt(window(extended, 0, block), queries)
        dweights = dot_nt(window(extended, 1, block), cotangent)
        return queries, cotangent, scores, dweights

    def softmax(block, queries, cotangent, scores, dweights):
        row = lax.broadcasted_iota(jnp.int32, (BLOCK, BLOCK), 0)
        col = lax.broadcasted_iota(jnp.int32, (BLOCK, BLOCK), 1)
        scores = jnp.concatenate(
            [
                without_absent(scores[:BLOCK], block, 1, BLOCK, is_first),
                jnp.where(row <= col, scores[BLOCK : 2 * BLOCK], NEG),
                without_absent(scores[2 * BLOCK : 3 * BLOCK], block, 3, HALF, is_first),
                without_absent(scores[3 * BLOCK :], block, 7, QUARTER, is_first),
            ],
            axis=0,
        )
        top = jnp.max(scores, axis=0, keepdims=True)
        powers = jnp.exp2((scores - top) * (SCALE * LOG2E))
        norm = 1.0 / jnp.sum(powers, axis=0, keepdims=True)
        delta = jnp.sum(powers * dweights, axis=0, keepdims=True) * norm
        weights = powers * norm
        dscores = weights * (dweights - delta)
        return queries, cotangent, weights.astype(jnp.bfloat16), dscores.astype(jnp.bfloat16)

    def results(block, queries, cotangent, weights, dscores):
        step, inner = block // local, block % local
        attended = dot_tn(window(extended, 1, block), weights)
        dqueries = dot_tn(window(extended, 0, block), dscores) * SCALE
        store_rows(out, 0, step, inner, jnp.transpose(attended).astype(jnp.bfloat16))
        store_rows(out, 1, step, inner, jnp.transpose(dqueries).astype(jnp.bfloat16))
        dkeys = dot_nn(dscores, queries) * SCALE
        dvalues = dot_nn(weights, cotangent)
        for kv, grads in enumerate((dkeys, dvalues)):
            before, here = grads[:BLOCK], grads[BLOCK : 2 * BLOCK]
            pairs, fours = grads[2 * BLOCK : 3 * BLOCK], grads[3 * BLOCK :]
            total[kv, block * BLOCK : (block + 1) * BLOCK] = here
            if block == 0:
                edge[kv] = before
                mgrad[kv, : 2 * HALF] = pairs
                rgrad[kv, : 4 * QUARTER] = fours
                continue
            total[kv, (block - 1) * BLOCK : block * BLOCK] += before
            mgrad[kv, block * HALF : (block + 1) * HALF] += pairs[:HALF]
            mgrad[kv, (block + 1) * HALF : (block + 2) * HALF] = pairs[HALF:]
            rgrad[kv, block * QUARTER : (block + 3) * QUARTER] += fours[: 3 * QUARTER]
            rgrad[kv, (block + 3) * QUARTER : (block + 4) * QUARTER] = fours[3 * QUARTER :]

    ahead = products(0)
    behind = None
    for block in range(blocks):
        current = ahead
        if block + 1 < blocks:
            ahead = products(block + 1)
        finished = softmax(block, *current)
        if behind is not None:
            results(block - 1, *behind)
        behind = finished
    results(blocks - 1, *behind)

    for kv in range(2):
        pairs = mgrad[kv, 2 * HALF :] * 0.5
        for lane in range(2):
            edge[kv, pl.ds(lane, HALF, stride=2), :] += pairs[:HALF]
            total[kv, pl.ds(lane, (blocks - 2) * HALF, stride=2), :] += pairs[HALF:]
        fours = rgrad[kv, 6 * QUARTER :] * 0.25
        for lane in range(4):
            edge[kv, pl.ds(lane, QUARTER, stride=4), :] += fours[:QUARTER]
            total[kv, pl.ds(lane, (blocks - 4) * QUARTER, stride=4), :] += fours[QUARTER:]
        shares = rgrad[kv, 4 * QUARTER : 6 * QUARTER] * 0.5
        for lane in range(2):
            mgrad[kv, pl.ds(lane, 2 * QUARTER, stride=2), :] += shares
        back[kv, :BLOCK] = edge[kv].astype(jnp.bfloat16)
        back[kv, BLOCK : BLOCK + 2 * HALF] = mgrad[kv, : 2 * HALF].astype(jnp.bfloat16)
        back[kv, BLOCK + 2 * HALF :] = rgrad[kv, : 4 * QUARTER].astype(jnp.bfloat16)


def attend(first_group, moved, moved_kv, halo):
    blocks, local, per_block, rows = sizes(moved)
    f32 = jnp.float32
    return pl.pallas_call(
        attend_body,
        out_shape=(
            jax.ShapeDtypeStruct((moved.shape[0], 4) + moved.shape[2:], moved.dtype),
            jax.ShapeDtypeStruct((2, blocks * BLOCK, HD), f32),
            jax.ShapeDtypeStruct((2, BACK, HD), jnp.bfloat16),
        ),
        in_specs=[pl.BlockSpec(memory_space=pltpu.SMEM)] + whole(3),
        out_specs=tuple(whole(3)),
        scratch_shapes=[
            pltpu.VMEM((2, (blocks + 1) * BLOCK, HD), jnp.bfloat16),
            pltpu.VMEM((2, (blocks + 3) * HALF, HD), jnp.bfloat16),
            pltpu.VMEM((2, (blocks + 7) * QUARTER, HD), jnp.bfloat16),
            pltpu.VMEM((2, BLOCK, HD), f32),
            pltpu.VMEM((2, (blocks + 1) * HALF, HD), f32),
            pltpu.VMEM((2, (blocks + 3) * QUARTER, HD), f32),
        ],
        compiler_params=params(24),
        cost_estimate=cost(blocks * 12 * BLOCK * 4 * BLOCK * HD, 8 * 2**20),
    )(first_group, moved, moved_kv, halo)


def finish_body(total, back, given, out, scratch):
    out[:, :2] = given[:, :2]
    sources, _, local, rows, _ = out.shape
    per_block = BLOCK // rows
    blocks = sources // per_block * local
    for kv in range(2):
        scratch[...] = total[kv]
        last = (blocks - 1) * BLOCK
        scratch[last:] += back[kv, :BLOCK].astype(jnp.float32)
        pairs = back[kv, BLOCK : BLOCK + 2 * HALF].astype(jnp.float32) * 0.5
        for lane in range(2):
            at = pl.ds((blocks - 3) * BLOCK + lane, 2 * HALF, stride=2)
            scratch[at, :] += pairs
        fours = back[kv, BLOCK + 2 * HALF :].astype(jnp.float32) * 0.25
        for lane in range(4):
            at = pl.ds((blocks - 7) * BLOCK + lane, 4 * QUARTER, stride=4)
            scratch[at, :] += fours
        for source in range(sources):
            for inner in range(local):
                start = (source // per_block * local + inner) * BLOCK + source % per_block * rows
                piece = scratch[start : start + rows].astype(jnp.bfloat16)
                out[source, 2 + kv, inner] = piece


def finish(total, back, out):
    return pl.pallas_call(
        finish_body,
        out_shape=jax.ShapeDtypeStruct(out.shape, out.dtype),
        in_specs=whole(2) + [pl.BlockSpec(memory_space=pltpu.VMEM)],
        out_specs=whole(1)[0],
        scratch_shapes=[pltpu.VMEM(total.shape[1:], jnp.float32)],
        input_output_aliases={2: 0},
        compiler_params=params(12),
        cost_estimate=cost(0, total.size * 6),
    )(total, back, out)


def exchange(parts):
    return lax.all_to_all(parts, GROUP_AXES, split_axis=0, concat_axis=0, tiled=True)


def shifted(block, distance):
    devices = range(lax.axis_size("seq"))
    route = [(i - distance, i) for i in devices if i - distance in devices]
    return lax.ppermute(block, "seq", route)


def shards(queries, keys, values, cotangent):
    first_group = (lax.axis_index("seq") == 0).astype(jnp.int32).reshape(1)
    with jax.named_scope("keys_in"):
        moved_kv = exchange(spread(keys, values))
    with jax.named_scope("queries_in"):
        sent, moved_kv = lax.optimization_barrier((spread(queries, cotangent), moved_kv))
        moved = exchange(sent)
    with jax.named_scope("halo"):
        halo = shifted(message(moved_kv), 1)
    with jax.named_scope("attend"):
        out, total, back = attend(first_group, moved, moved_kv, halo)
    with jax.named_scope("halo_back"):
        out = finish(total, shifted(back, -1), out)
    with jax.named_scope("outputs"):
        return join(exchange(out))


def solution(mesh):
    spec = P(("seq", "ctx"), "head", None)
    return jax.shard_map(
        shards, mesh=mesh, in_specs=(spec,) * 4, out_specs=(spec,) * 4, check_vma=False
    )
```

```python
import functools
import math

import jax
import jax.numpy as jnp
from jax import lax
from jax.experimental import pallas as pl
from jax.experimental.pallas import tpu as pltpu
from jax.sharding import PartitionSpec as P

HD = 128
BLOCK = 256
HALF = BLOCK // 2
QUARTER = BLOCK // 4
SCALE = 1.0 / math.sqrt(HD)
LOG2E = 1.0 / math.log(2.0)
NEG = -1e30
HALO_FINE = BLOCK
HALO_MID = 2 * HALF
HALO_FAR = 6 * QUARTER
HALO = HALO_FINE + HALO_MID + HALO_FAR
BACK = BLOCK + 2 * HALF + 4 * QUARTER
GROUP_AXES = ("ctx", "head")


def whole(count):
    return [pl.BlockSpec(memory_space=pltpu.VMEM)] * count


def params(mebibytes):
    return pltpu.CompilerParams(vmem_limit_bytes=mebibytes * 2**20)


def cost(flops, nbytes):
    return pl.CostEstimate(flops=flops, bytes_accessed=nbytes, transcendentals=0)


def spread_body(*refs):
    count = (len(refs) - 2) // 3
    sources, out = refs[:count], refs[count]
    held, turned, sems = refs[count + 1 : 2 * count + 1], refs[2 * count + 1 : -1], refs[-1]
    heads, _, blocks, _, _ = out.shape
    fetches = {}
    for which in range(count):
        for block in range(blocks):
            fetches[which, block] = pltpu.make_async_copy(
                sources[which].at[block], held[which].at[block], sems.at[which, block]
            )
            fetches[which, block].start()
    sends = []
    for which in range(count):
        for block in range(blocks):
            fetches[which, block].wait()
            for head in range(heads):
                turned[which][head, block] = held[which][block, :, head * HD : (head + 1) * HD]
        send = pltpu.make_async_copy(turned[which], out.at[:, which], sems.at[which, blocks])
        send.start()
        sends.append(send)
    for send in sends:
        send.wait()


def spread(*arrays):
    blocks, rows, features = arrays[0].shape
    heads = features // HD
    count = len(arrays)
    kind = arrays[0].dtype
    there = pl.BlockSpec(memory_space=pltpu.HBM)
    return pl.pallas_call(
        spread_body,
        out_shape=jax.ShapeDtypeStruct((heads, count, blocks, rows, HD), kind),
        in_specs=[there] * count,
        out_specs=there,
        scratch_shapes=[pltpu.VMEM((blocks, rows, features), kind)] * count
        + [pltpu.VMEM((heads, blocks, rows, HD), kind)] * count
        + [pltpu.SemaphoreType.DMA((count, blocks + 1))],
        compiler_params=params(58),
        cost_estimate=cost(0, 4 * count * arrays[0].size),
    )(*arrays)


def join_body(moved, *outs):
    block, part = pl.program_id(0), pl.program_id(1)
    rows = outs[0].shape[1]
    at = pl.ds(pl.multiple_of(part * rows, rows), rows)
    for which, out in enumerate(outs):
        for head in range(moved.shape[0]):
            out[0, :, head * HD : (head + 1) * HD] = moved[head, which, block, at]


def join(moved):
    heads, count, blocks, rows, _ = moved.shape
    out = jax.ShapeDtypeStruct((blocks, rows, heads * HD), moved.dtype)
    one = pl.BlockSpec((1, rows // 2, heads * HD), lambda block, part: (block, part, 0))
    return pl.pallas_call(
        join_body,
        grid=(blocks, 2),
        out_shape=(out,) * count,
        in_specs=whole(1),
        out_specs=(one,) * count,
        compiler_params=params(8),
        cost_estimate=cost(0, 4 * moved.size),
    )(moved)


def pool_matrix():
    row = lax.broadcasted_iota(jnp.int32, (HALF + QUARTER, BLOCK), 0)
    col = lax.broadcasted_iota(jnp.int32, (HALF + QUARTER, BLOCK), 1)
    pair = (row < HALF) & ((col >> 1) == row)
    four = (row >= HALF) & ((col >> 2) == row - HALF)
    both = jnp.where(pair, 0.5, 0.0) + jnp.where(four, 0.25, 0.0)
    return both.astype(jnp.bfloat16)


def sizes(moved):
    sources, _, local, rows, _ = moved.shape
    per_block = BLOCK // rows
    return sources // per_block * local, local, per_block, rows


def tokens_of(moved, which, step, inner):
    per_block = BLOCK // moved.shape[3]
    return jnp.concatenate(
        [moved[step * per_block + part, which, inner] for part in range(per_block)], axis=0
    )


def places(block):
    return (
        pl.ds(block * BLOCK, 2 * BLOCK),
        pl.ds(block * HALF, 2 * HALF),
        pl.ds(block * QUARTER, 4 * QUARTER),
    )


def window(extended, kv, block):
    return jnp.concatenate([ref[kv, at] for ref, at in zip(extended, places(block))], axis=0)


def store_rows(out, which, step, inner, value):
    rows = out.shape[3]
    per_block = BLOCK // rows
    for part in range(per_block):
        out[step * per_block + part, which, inner] = value[part * rows : (part + 1) * rows]


def pooled_rows(matrix, tokens):
    return jnp.dot(matrix, tokens, preferred_element_type=jnp.float32).astype(jnp.bfloat16)


def message_body(moved, msg):
    blocks, local, _, _ = sizes(moved)
    matrix = pool_matrix()
    for kv in range(2):
        for from_end in range(1, 8):
            block = blocks - from_end
            tokens = tokens_of(moved, kv, block // local, block % local)
            if from_end == 1:
                msg[kv, :HALO_FINE] = tokens
                continue
            pooled = pooled_rows(matrix, tokens)
            if from_end <= 3:
                start = HALO_FINE + (3 - from_end) * HALF
                msg[kv, start : start + HALF] = pooled[:HALF]
            start = HALO_FINE + HALO_MID + (7 - from_end) * QUARTER
            msg[kv, start : start + QUARTER] = pooled[HALF:]


def message(moved):
    return pl.pallas_call(
        message_body,
        out_shape=jax.ShapeDtypeStruct((2, HALO, HD), jnp.bfloat16),
        in_specs=whole(1),
        out_specs=whole(1)[0],
        compiler_params=params(8),
        cost_estimate=cost(4 * 6 * 192 * BLOCK * HD, moved.size * 2),
    )(moved)


def dot_nt(a, b):
    return lax.dot_general(a, b, (((1,), (1,)), ((), ())), preferred_element_type=jnp.float32)


def dot_tn(a, b):
    return lax.dot_general(a, b, (((0,), (0,)), ((), ())), preferred_element_type=jnp.float32)


def dot_nn(a, b):
    return jnp.dot(a, b, preferred_element_type=jnp.float32)


def extend(moved, halo, fext, mext, rext):
    blocks, local, _, _ = sizes(moved)
    matrix = pool_matrix()
    for kv in range(2):
        mext[kv, : 2 * HALF] = halo[kv, HALO_FINE : HALO_FINE + HALO_MID]
        rext[kv, : 6 * QUARTER] = halo[kv, HALO_FINE + HALO_MID :]
        for block in range(-1, blocks):
            if block < 0:
                tokens = halo[kv, :HALO_FINE]
            else:
                tokens = tokens_of(moved, kv, block // local, block % local)
            pooled = pooled_rows(matrix, tokens)
            fext[kv, (block + 1) * BLOCK : (block + 2) * BLOCK] = tokens
            mext[kv, (block + 3) * HALF : (block + 4) * HALF] = pooled[:HALF]
            rext[kv, (block + 7) * QUARTER : (block + 8) * QUARTER] = pooled[HALF:]


def without_absent(piece, block, offset, rows, is_first):
    count = min(max(offset - block, 0) * rows, BLOCK)
    if count == 0:
        return piece
    row = lax.broadcasted_iota(jnp.int32, (count, BLOCK), 0)
    masked = jnp.where(row < is_first * count, NEG, piece[:count])
    return masked if count == BLOCK else jnp.concatenate([masked, piece[count:]], axis=0)


def attend_body(
    first_group,
    moved,
    moved_kv,
    halo,
    out,
    total,
    back,
    fext,
    mext,
    rext,
    edge,
    mgrad,
    rgrad,
):
    blocks, local, _, _ = sizes(moved)
    extend(moved_kv, halo, fext, mext, rext)
    is_first = first_group[0]
    extended = (fext, mext, rext)

    def products(block):
        queries = tokens_of(moved, 0, block // local, block % local)
        cotangent = tokens_of(moved, 1, block // local, block % local)
        scores = dot_nt(window(extended, 0, block), queries)
        dweights = dot_nt(window(extended, 1, block), cotangent)
        return queries, cotangent, scores, dweights

    def softmax(block, queries, cotangent, scores, dweights):
        row = lax.broadcasted_iota(jnp.int32, (BLOCK, BLOCK), 0)
        col = lax.broadcasted_iota(jnp.int32, (BLOCK, BLOCK), 1)
        scores = jnp.concatenate(
            [
                without_absent(scores[:BLOCK], block, 1, BLOCK, is_first),
                jnp.where(row <= col, scores[BLOCK : 2 * BLOCK], NEG),
                without_absent(scores[2 * BLOCK : 3 * BLOCK], block, 3, HALF, is_first),
                without_absent(scores[3 * BLOCK :], block, 7, QUARTER, is_first),
            ],
            axis=0,
        )
        top = jnp.max(scores, axis=0, keepdims=True)
        powers = jnp.exp2((scores - top) * (SCALE * LOG2E))
        norm = 1.0 / jnp.sum(powers, axis=0, keepdims=True)
        delta = jnp.sum(powers * dweights, axis=0, keepdims=True) * norm
        weights = powers * norm
        dscores = weights * (dweights - delta)
        return queries, cotangent, weights.astype(jnp.bfloat16), dscores.astype(jnp.bfloat16)

    def results(block, queries, cotangent, weights, dscores):
        step, inner = block // local, block % local
        attended = dot_tn(window(extended, 1, block), weights)
        dqueries = dot_tn(window(extended, 0, block), dscores) * SCALE
        store_rows(out, 0, step, inner, jnp.transpose(attended).astype(jnp.bfloat16))
        store_rows(out, 1, step, inner, jnp.transpose(dqueries).astype(jnp.bfloat16))
        dkeys = dot_nn(dscores, queries) * SCALE
        dvalues = dot_nn(weights, cotangent)
        for kv, grads in enumerate((dkeys, dvalues)):
            before, here = grads[:BLOCK], grads[BLOCK : 2 * BLOCK]
            pairs, fours = grads[2 * BLOCK : 3 * BLOCK], grads[3 * BLOCK :]
            total[kv, block * BLOCK : (block + 1) * BLOCK] = here
            if block == 0:
                edge[kv] = before
                mgrad[kv, : 2 * HALF] = pairs
                rgrad[kv, : 4 * QUARTER] = fours
                continue
            total[kv, (block - 1) * BLOCK : block * BLOCK] += before
            mgrad[kv, block * HALF : (block + 1) * HALF] += pairs[:HALF]
            mgrad[kv, (block + 1) * HALF : (block + 2) * HALF] = pairs[HALF:]
            rgrad[kv, block * QUARTER : (block + 3) * QUARTER] += fours[: 3 * QUARTER]
            rgrad[kv, (block + 3) * QUARTER : (block + 4) * QUARTER] = fours[3 * QUARTER :]

    ahead = products(0)
    behind = None
    for block in range(blocks):
        current = ahead
        if block + 1 < blocks:
            ahead = products(block + 1)
        finished = softmax(block, *current)
        if behind is not None:
            results(block - 1, *behind)
        behind = finished
    results(blocks - 1, *behind)

    for kv in range(2):
        pairs = mgrad[kv, 2 * HALF :] * 0.5
        for lane in range(2):
            edge[kv, pl.ds(lane, HALF, stride=2), :] += pairs[:HALF]
            total[kv, pl.ds(lane, (blocks - 2) * HALF, stride=2), :] += pairs[HALF:]
        fours = rgrad[kv, 6 * QUARTER :] * 0.25
        for lane in range(4):
            edge[kv, pl.ds(lane, QUARTER, stride=4), :] += fours[:QUARTER]
            total[kv, pl.ds(lane, (blocks - 4) * QUARTER, stride=4), :] += fours[QUARTER:]
        shares = rgrad[kv, 4 * QUARTER : 6 * QUARTER] * 0.5
        for lane in range(2):
            mgrad[kv, pl.ds(lane, 2 * QUARTER, stride=2), :] += shares
        back[kv, :BLOCK] = edge[kv].astype(jnp.bfloat16)
        back[kv, BLOCK : BLOCK + 2 * HALF] = mgrad[kv, : 2 * HALF].astype(jnp.bfloat16)
        back[kv, BLOCK + 2 * HALF :] = rgrad[kv, : 4 * QUARTER].astype(jnp.bfloat16)


def attend(first_group, moved, moved_kv, halo):
    blocks, local, per_block, rows = sizes(moved)
    f32 = jnp.float32
    return pl.pallas_call(
        attend_body,
        out_shape=(
            jax.ShapeDtypeStruct((moved.shape[0], 4) + moved.shape[2:], moved.dtype),
            jax.ShapeDtypeStruct((2, blocks * BLOCK, HD), f32),
            jax.ShapeDtypeStruct((2, BACK, HD), jnp.bfloat16),
        ),
        in_specs=[pl.BlockSpec(memory_space=pltpu.SMEM)] + whole(3),
        out_specs=tuple(whole(3)),
        scratch_shapes=[
            pltpu.VMEM((2, (blocks + 1) * BLOCK, HD), jnp.bfloat16),
            pltpu.VMEM((2, (blocks + 3) * HALF, HD), jnp.bfloat16),
            pltpu.VMEM((2, (blocks + 7) * QUARTER, HD), jnp.bfloat16),
            pltpu.VMEM((2, BLOCK, HD), f32),
            pltpu.VMEM((2, (blocks + 1) * HALF, HD), f32),
            pltpu.VMEM((2, (blocks + 3) * QUARTER, HD), f32),
        ],
        compiler_params=params(24),
        cost_estimate=cost(blocks * 12 * BLOCK * 4 * BLOCK * HD, 8 * 2**20),
    )(first_group, moved, moved_kv, halo)


def finish_body(total, back, given, out, scratch):
    out[:, :2] = given[:, :2]
    sources, _, local, rows, _ = out.shape
    per_block = BLOCK // rows
    blocks = sources // per_block * local
    for kv in range(2):
        scratch[...] = total[kv]
        last = (blocks - 1) * BLOCK
        scratch[last:] += back[kv, :BLOCK].astype(jnp.float32)
        pairs = back[kv, BLOCK : BLOCK + 2 * HALF].astype(jnp.float32) * 0.5
        for lane in range(2):
            at = pl.ds((blocks - 3) * BLOCK + lane, 2 * HALF, stride=2)
            scratch[at, :] += pairs
        fours = back[kv, BLOCK + 2 * HALF :].astype(jnp.float32) * 0.25
        for lane in range(4):
            at = pl.ds((blocks - 7) * BLOCK + lane, 4 * QUARTER, stride=4)
            scratch[at, :] += fours
        for source in range(sources):
            for inner in range(local):
                start = (source // per_block * local + inner) * BLOCK + source % per_block * rows
                piece = scratch[start : start + rows].astype(jnp.bfloat16)
                out[source, 2 + kv, inner] = piece


def finish(total, back, out):
    return pl.pallas_call(
        finish_body,
        out_shape=jax.ShapeDtypeStruct(out.shape, out.dtype),
        in_specs=whole(2) + [pl.BlockSpec(memory_space=pltpu.VMEM)],
        out_specs=whole(1)[0],
        scratch_shapes=[pltpu.VMEM(total.shape[1:], jnp.float32)],
        input_output_aliases={2: 0},
        compiler_params=params(12),
        cost_estimate=cost(0, total.size * 6),
    )(total, back, out)


def exchange(parts):
    return lax.all_to_all(parts, GROUP_AXES, split_axis=0, concat_axis=0, tiled=True)


def shifted(block, distance):
    devices = range(lax.axis_size("seq"))
    route = [(i - distance, i) for i in devices if i - distance in devices]
    return lax.ppermute(block, "seq", route)


def shards(queries, keys, values, cotangent):
    first_group = (lax.axis_index("seq") == 0).astype(jnp.int32).reshape(1)
    with jax.named_scope("keys_in"):
        moved_kv = exchange(spread(keys, values))
    with jax.named_scope("queries_in"):
        sent, moved_kv = lax.optimization_barrier((spread(queries, cotangent), moved_kv))
        moved = exchange(sent)
    with jax.named_scope("halo"):
        halo = shifted(message(moved_kv), 1)
    with jax.named_scope("attend"):
        out, total, back = attend(first_group, moved, moved_kv, halo)
    with jax.named_scope("halo_back"):
        out = finish(total, shifted(back, -1), out)
    with jax.named_scope("outputs"):
        return join(exchange(out))


def solution(mesh):
    spec = P(("seq", "ctx"), "head", None)
    return jax.shard_map(
        shards, mesh=mesh, in_specs=(spec,) * 4, out_specs=(spec,) * 4, check_vma=False
    )
```
